256 devices in a mesh: tm: 16 (over x, y_hi, core), space: 16 (over y_lo, z).
Axes of the slice: x: 4, y: 4 (y_hi: 2, y_lo: 2; y = y_hi * 2 + y_lo), z: 8, core: 2. Of those that a mesh axis runs over, the one named last changes fastest.
Arguments:
- state: float32 [32, 128, 64, 256], P('tm', 'space'), may hold values from -1.5 to 1.5
- initial: float32 [128, 64, 256], P('space'), may hold values from -1.5 to 1.5
Outputs:
- updated: float32 [32, 128, 64, 256], P('tm', 'space')
- residual: float32 [32, 128, 64, 256], P('tm', 'space')
The draws below stay inside these ranges and needn't reach their ends.
All inputs are finite; a program needn't handle non-finite values.
Results may differ from the reference program's by a relative error of at most 0.0003.
Values sent between devices are 32-bit elements; how exact they have to be, the bound alone decides.
A program may use at most 64 MiB of HBM per device.

```python
import math
import jax
import jax.numpy as jnp
from jax import lax

NY = 64
NZ = 256
SWEEPS = 6
STEPS = 32
NX = 128


def draw_state(key, part):
    shape = (STEPS, NX, NY, NZ)
    return jax.random.uniform(key, shape, jnp.float32, -1.5, 1.5)


def block_levels(key, dims, split, low, largest):
    loudness, own = 1.0, jax.random.fold_in(key, 6)
    for axis_at, shards_of in split:
        steps = jnp.exp(jax.random.uniform(jax.random.fold_in(own, axis_at), (shards_of,), jnp.float32, low / len(split), largest / len(split)))
        loudness = loudness * jnp.repeat(steps, dims[axis_at] // shards_of).reshape([-1 if axis == axis_at else 1 for axis in range(len(dims))])
    return loudness


def setup_inputs(seed: int = 0) -> dict:
    seeds = jax.random.split(jax.random.key(seed), 3)
    state = draw_state(jax.random.fold_in(seeds[2], 71), 0)
    initial = jnp.clip(jax.random.uniform(seeds[1], (NX, NY, NZ), jnp.float32, -1.5, 1.5) * block_levels(seeds[1], (NX, NY, NZ), ((0, 16),), -0.4, 0.0), -1.5, 1.5)
    return dict(state=state, initial=initial)


alpha_value = 0.1
time_step = 0.1
couple_first = 0.4
couple_cross = 0.05
reaction_shift = 0.1
relaxation = 0.9


def first_sum(field):
    return jnp.roll(field, 1, -3) + jnp.roll(field, -1, -3)


def cross_sum(field):
    return (jnp.roll(field, 1, -2) + jnp.roll(field, -1, -2)
            + jnp.roll(field, 1, -1) + jnp.roll(field, -1, -1))


def phases(lefts, rights, horizon):
    products = (lefts[:, None] * rights[None, :]) % horizon
    return (2.0 * math.pi / horizon) * products.astype(jnp.float32)


def scales(horizon):
    counter = jnp.arange(horizon)
    return jnp.power(alpha_value, counter.astype(jnp.float32) / horizon)


def mode_diagonal(modes, horizon):
    root_alpha = alpha_value ** (1.0 / horizon)
    angles = (2.0 * math.pi / horizon) * modes.astype(jnp.float32)
    diag_real = 1.0 - root_alpha * jnp.cos(angles) + reaction_shift + 2.0 * couple_first + 4.0 * couple_cross
    diag_imag = root_alpha * jnp.sin(angles)
    return diag_real, diag_imag


def reference(state, initial):
    horizon = state.shape[0]
    before = jnp.concatenate([initial[None], state[:-1]], axis=0)
    laplace = couple_first * (first_sum(state) - 2.0 * state) + couple_cross * (cross_sum(state) - 4.0 * state)
    residual = before - state + laplace + time_step * (state - state * state * state)
    counter = jnp.arange(horizon)
    angles = phases(counter, counter, horizon)
    weight = scales(horizon)
    fore_cos = jnp.cos(angles) * weight[None, :]
    fore_sin = -jnp.sin(angles) * weight[None, :]
    back_cos = jnp.cos(angles).T / (horizon * weight[:, None])
    back_sin = -jnp.sin(angles).T / (horizon * weight[:, None])
    highest = lax.Precision.HIGHEST
    spec_real = jnp.einsum('kn,nxyz->kxyz', fore_cos, residual, precision=highest)
    spec_imag = jnp.einsum('kn,nxyz->kxyz', fore_sin, residual, precision=highest)
    diag_real, diag_imag = mode_diagonal(counter, horizon)
    magnitude = diag_real * diag_real + diag_imag * diag_imag
    inv_real = diag_real / magnitude
    inv_imag = -diag_imag / magnitude

    def solve_mode(operands):
        source_real, source_imag, real_part, imag_part = operands
        solved_real = relaxation * (real_part * source_real - imag_part * source_imag)
        solved_imag = relaxation * (real_part * source_imag + imag_part * source_real)
        for sweep_index in range(SWEEPS - 1):
            total_real = source_real + (couple_first * first_sum(solved_real) + couple_cross * cross_sum(solved_real))
            total_imag = source_imag + (couple_first * first_sum(solved_imag) + couple_cross * cross_sum(solved_imag))
            solved_real, solved_imag = (
                (1.0 - relaxation) * solved_real + relaxation * (real_part * total_real - imag_part * total_imag),
                (1.0 - relaxation) * solved_imag + relaxation * (imag_part * total_real + real_part * total_imag))
        return solved_real, solved_imag

    solved_real, solved_imag = lax.map(solve_mode, (spec_real, spec_imag, inv_real, inv_imag))
    delta = (jnp.einsum('nk,kxyz->nxyz', back_cos, solved_real, precision=highest)
             + jnp.einsum('nk,kxyz->nxyz', back_sin, solved_imag, precision=highest))
    return state + delta, residual
```

```python
import math

import jax
import jax.numpy as jnp
import ml_dtypes
import numpy as np
from jax import lax
from jax.experimental import pallas as pl
from jax.experimental.pallas import tpu as pltpu
from jax.sharding import PartitionSpec as P

MESH = pl.DeviceIdType.MESH
SWEEPS = 6
STEPS, NX, NY, NZ = 32, 128, 64, 256
ROWS = 16
RING = 16
SLAB = NX // RING
REACH = SWEEPS - 1
WIDE = SLAB + 2 * REACH
SUB, LANE = 8, 128
CHUNKS = 2

alpha_value = 0.1
time_step = 0.1
couple_first = 0.4
couple_cross = 0.05
reaction_shift = 0.1
relaxation = 0.9
rho = alpha_value ** (1.0 / STEPS)


def real_basis(n):
    cells = np.arange(n)
    rows, freq = np.zeros((n, n)), np.zeros(n)
    rows[0] = 1.0 / math.sqrt(n)
    rows[1] = (-1.0) ** cells / math.sqrt(n)
    freq[1] = n // 2
    for k in range(1, n // 2):
        angle = 2.0 * math.pi * (k * cells % n) / n
        rows[2 * k] = math.sqrt(2.0 / n) * np.cos(angle)
        rows[2 * k + 1] = math.sqrt(2.0 / n) * np.sin(angle)
        freq[2 * k] = freq[2 * k + 1] = k
    return rows, freq


def halves(matrix):
    high = matrix.astype(ml_dtypes.bfloat16)
    low = (matrix - high.astype(np.float64)).astype(ml_dtypes.bfloat16)
    return high, low


def mode_factors(k):
    theta = 2.0 * math.pi * k / STEPS
    diag = 1.0 + reaction_shift + 2.0 * couple_first + 4.0 * couple_cross
    shift = complex(diag - rho * math.cos(theta), rho * math.sin(theta))
    scale = relaxation / shift
    beta = couple_first * scale
    roots = [complex(np.exp(2j * math.pi * j / SWEEPS)) for j in range(1, SWEEPS)]
    return [(1.0 - relaxation - root) / beta for root in roots], beta**REACH * scale


def constants():
    basis_z, freq_z = real_basis(NZ)
    basis_y, freq_y = real_basis(NY)
    wave_z = 2.0 * np.cos(2.0 * math.pi * freq_z / NZ)
    wave_y = 2.0 * np.cos(2.0 * math.pi * freq_y / NY)
    mu = (couple_cross / couple_first) * (wave_y[:, None] + wave_z[None, :])
    mu = mu.reshape(NY // SUB, SUB, NZ // LANE, LANE).transpose(0, 2, 1, 3)
    mu = mu.reshape(ROWS, SUB, LANE).astype(np.float32)
    zf = np.stack(halves(basis_z.T))
    zb = np.stack(halves(basis_z))
    yh, yl = halves(basis_y)
    yf = np.concatenate([yh, yh, yl], axis=1)
    yh, yl = halves(basis_y.T)
    yb = np.concatenate([yh, yh, yl], axis=1)
    table = []
    for k in range(1, STEPS // 2):
        factors, last = mode_factors(k)
        for value in factors + [last]:
            table += [value.real, value.imag]
    return mu, zf, zb, np.stack([yf, yb]), np.asarray(table, np.float32)


def split(value):
    high = value.astype(jnp.bfloat16)
    low = (value - high.astype(jnp.float32)).astype(jnp.bfloat16)
    return high, low


def dot(a, b):
    return jnp.dot(a, b, preferred_element_type=jnp.float32)


def rfft(x):
    n = len(x)
    if n == 2:
        return [(x[0] + x[1], None), (x[0] - x[1], None)]
    even, odd = rfft(x[0::2]), rfft(x[1::2])
    h, q = n // 2, n // 4
    out = [None] * (h + 1)
    out[0] = (even[0][0] + odd[0][0], None)
    out[h] = (even[0][0] - odd[0][0], None)
    out[q] = (even[q][0], -odd[q][0])
    for k in range(1, q):
        c, s = math.cos(2.0 * math.pi * k / n), -math.sin(2.0 * math.pi * k / n)
        er, ei = even[k]
        pr, pi = odd[k]
        tr, ti = c * pr - s * pi, c * pi + s * pr
        out[k] = (er + tr, ei + ti)
        out[h - k] = (er - tr, ti - ei)
    return out


def irfft(modes):
    n = 2 * (len(modes) - 1)
    if n == 2:
        return [modes[0][0] + modes[1][0], modes[0][0] - modes[1][0]]
    h, q = n // 2, n // 4
    even, odd = [None] * (q + 1), [None] * (q + 1)
    even[0] = (modes[0][0] + modes[h][0], None)
    odd[0] = (modes[0][0] - modes[h][0], None)
    even[q] = (2.0 * modes[q][0], None)
    odd[q] = (-2.0 * modes[q][1], None)
    for k in range(1, q):
        c, s = math.cos(2.0 * math.pi * k / n), math.sin(2.0 * math.pi * k / n)
        ar, ai = modes[k]
        br, bi = modes[h - k]
        even[k] = (ar + br, ai - bi)
        dr, di = ar - br, ai + bi
        odd[k] = (c * dr - s * di, c * di + s * dr)
    out = [None] * n
    out[0::2], out[1::2] = irfft(even), irfft(odd)
    return out


def kernel(
    state, initial, mu_ref, zf, zb, ymat, table,
    updated, residual,
    st, bef, res, upd, fore, mid, spec, back, ret, row_hi, row_lo,
    local_sem, edge_send, edge_recv, slab_send, slab_recv,
    fore_send, fore_recv, halo_send, halo_recv, back_send, back_recv,
):
    tm, sp = lax.axis_index("tm"), lax.axis_index("space")
    up, down = lax.rem(sp + 1, RING), lax.rem(sp + RING - 1, RING)

    def remote(src, dst, send, recv, device):
        return pltpu.make_async_remote_copy(
            src_ref=src, dst_ref=dst, send_sem=send, recv_sem=recv,
            device_id=device, device_id_type=MESH,
        )

    barrier = pltpu.get_barrier_semaphore()
    pl.semaphore_signal(barrier, inc=1, device_id=(tm, up), device_id_type=MESH)
    pl.semaphore_signal(barrier, inc=1, device_id=(tm, down), device_id_type=MESH)
    for o in range(1, ROWS):
        pl.semaphore_signal(
            barrier, inc=1, device_id=(jnp.bitwise_xor(tm, o), sp), device_id_type=MESH
        )
    load = pltpu.make_async_copy(state, st.at[:, pl.ds(1, SLAB)], local_sem.at[0])
    load.start()
    load.wait()

    @pl.when(tm == 0)
    def _():
        first = pltpu.make_async_copy(initial, bef, local_sem.at[1])
        first.start()
        first.wait()

    pl.semaphore_wait(barrier, ROWS + 1)

    edges = [
        remote(st.at[:, SLAB], st.at[:, 0], edge_send.at[0], edge_recv.at[0], (tm, up)),
        remote(st.at[:, 1], st.at[:, SLAB + 1], edge_send.at[1], edge_recv.at[1], (tm, down)),
    ]
    for copy in edges:
        copy.start()
    slab = remote(
        st.at[1, pl.ds(1, SLAB)], bef, slab_send.at[0], slab_recv.at[0],
        (lax.rem(tm + 1, ROWS), sp),
    )

    @pl.when(tm < ROWS - 1)
    def _():
        slab.start()

    def own_part(step, x):
        s = st[step, x + 1]
        near = st[step, x] + st[step, x + 2]
        cross = (
            pltpu.roll(s, 1, 0) + pltpu.roll(s, NY - 1, 0)
            + pltpu.roll(s, 1, 1) + pltpu.roll(s, NZ - 1, 1)
        )
        laplace = couple_first * (near - 2.0 * s) + couple_cross * (cross - 4.0 * s)
        return laplace - s + time_step * (s - s * s * s)

    def along_y(which, value):
        high, low = split(value)
        return dot(ymat[which], jnp.concatenate([high, low, high], axis=0))

    def keep_rows(at, value):
        high, low = split(value)
        rows = pl.ds(pl.multiple_of(at * NY, NY), NY)
        row_hi[rows] = high
        row_lo[rows] = low

    def along_z(matrix):
        high = row_hi[...]
        return dot(high, matrix[0]) + dot(row_lo[...], matrix[0]) + dot(high, matrix[1])

    def transform(step):
        gamma = jnp.exp(
            jnp.full((SUB, LANE), (2 * tm + step).astype(jnp.float32) * (math.log(alpha_value) / STEPS))
        )
        rows = along_z(zf)
        for x in range(SLAB):
            for g in range(ROWS):
                r0, c0 = x * NY + (g // 2) * SUB, (g % 2) * LANE
                fore[g, step, x] = rows[r0 : r0 + SUB, c0 : c0 + LANE] * gamma

    def fore_copy(step, o):
        peer = jnp.bitwise_xor(tm, o)
        return peer, remote(
            fore.at[peer, step], mid.at[step, tm, pl.ds(REACH, SLAB)],
            fore_send.at[step, o], fore_recv.at[step, o], (peer, sp),
        )

    def send_fore(step):
        @pl.loop(1, ROWS)
        def _(o):
            fore_copy(step, o)[1].start()

        own = pltpu.make_async_copy(
            fore.at[tm, step], mid.at[step, tm, pl.ds(REACH, SLAB)], local_sem.at[2 + step]
        )
        own.start()
        return own

    @pl.loop(1, SLAB - 1)
    def _(x):
        value = own_part(1, x) + st[0, x + 1]
        res[1, x] = value
        keep_rows(x, along_y(0, value))

    for copy in edges:
        copy.wait_recv()
    for x in (0, SLAB - 1):
        value = own_part(1, x) + st[0, x + 1]
        res[1, x] = value
        keep_rows(x, along_y(0, value))
    transform(1)
    own_odd = send_fore(1)

    @pl.loop(0, SLAB)
    def _(x):
        res[0, x] = own_part(0, x)

    @pl.when(tm > 0)
    def _():
        slab.wait_recv()

    @pl.loop(0, SLAB)
    def _(x):
        value = res[0, x] + bef[x]
        res[0, x] = value
        keep_rows(x, along_y(0, value))

    transform(0)
    own_even = send_fore(0)
    out_res = pltpu.make_async_copy(res, residual, local_sem.at[4])
    out_res.start()

    def halo_copies(step):
        return [
            remote(
                mid.at[step, :, pl.ds(SLAB, REACH)], mid.at[step, :, pl.ds(0, REACH)],
                halo_send.at[step, 0], halo_recv.at[step, 0], (tm, up),
            ),
            remote(
                mid.at[step, :, pl.ds(REACH, REACH)], mid.at[step, :, pl.ds(REACH + SLAB, REACH)],
                halo_send.at[step, 1], halo_recv.at[step, 1], (tm, down),
            ),
        ]

    for step, own in ((1, own_odd), (0, own_even)):
        own.wait()

        @pl.loop(1, ROWS)
        def _(o):
            peer = jnp.bitwise_xor(tm, o)
            landing = mid.at[step, peer, pl.ds(REACH, SLAB)]
            remote(
                landing, landing, fore_send.at[step, o], fore_recv.at[step, o], (peer, sp)
            ).wait_recv()

        for copy in halo_copies(step):
            copy.start()

    def to_modes(x):
        modes = rfft([mid[n % 2, n // 2, x] for n in range(STEPS)])
        spec[0, x] = modes[0][0]
        spec[1, x] = modes[STEPS // 2][0]
        for k in range(1, STEPS // 2):
            spec[2 * k, x] = modes[k][0]
            spec[2 * k + 1, x] = modes[k][1]

    @pl.loop(REACH, REACH + SLAB)
    def _(x):
        to_modes(x)

    for step in (1, 0):
        for copy in halo_copies(step):
            copy.wait_recv()

    @pl.loop(0, REACH)
    def _(x):
        to_modes(x)

    @pl.loop(REACH + SLAB, WIDE)
    def _(x):
        to_modes(x)

    mu = mu_ref[tm]

    for slot, k in ((0, 0), (1, STEPS // 2)):
        factors, last = mode_factors(k)
        v = [spec[slot, x] for x in range(WIDE)]
        for j in (0, 1):
            dr, square = mu + factors[j].real, factors[j].imag ** 2
            first = [v[x - 1] + v[x + 1] + dr * v[x] for x in range(1, len(v) - 1)]
            v = [
                first[x - 1] + first[x + 1] + dr * first[x] + square * v[x + 1]
                for x in range(1, len(first) - 1)
            ]
        dr = mu + factors[2].real
        v = [v[x - 1] + v[x + 1] + dr * v[x] for x in range(1, len(v) - 1)]
        for x in range(SLAB):
            spec[slot, x] = last.real * v[x]

    @pl.loop(1, STEPS // 2)
    def _(k):
        base = (k - 1) * 2 * SWEEPS
        vr = [spec[2 * k, x] for x in range(WIDE)]
        vi = [spec[2 * k + 1, x] for x in range(WIDE)]
        for j in range(REACH):
            dr, di = mu + table[base + 2 * j], table[base + 2 * j + 1]
            inner = range(1, len(vr) - 1)
            vr, vi = (
                [vr[x - 1] + vr[x + 1] + dr * vr[x] - di * vi[x] for x in inner],
                [vi[x - 1] + vi[x + 1] + dr * vi[x] + di * vr[x] for x in inner],
            )
        lr, li = table[base + 2 * REACH], table[base + 2 * REACH + 1]
        for x in range(SLAB):
            spec[2 * k, x] = lr * vr[x] - li * vi[x]
            spec[2 * k + 1, x] = lr * vi[x] + li * vr[x]

    part = SLAB // CHUNKS

    def back_copy(chunk, o):
        peer = jnp.bitwise_xor(tm, o)
        xs = pl.ds(chunk * part, part)
        return remote(
            back.at[peer, :, xs], ret.at[tm, :, xs],
            back_send.at[chunk, o], back_recv.at[chunk, o], (peer, sp),
        )

    own_back = []
    for chunk in range(CHUNKS):
        @pl.loop(chunk * part, (chunk + 1) * part)
        def _(x):
            modes = [(spec[0, x], None)]
            modes += [(spec[2 * k, x], spec[2 * k + 1, x]) for k in range(1, STEPS // 2)]
            modes += [(spec[1, x], None)]
            values = irfft(modes)
            for n in range(STEPS):
                back[n // 2, n % 2, x] = values[n]

        @pl.loop(1, ROWS)
        def _(o):
            back_copy(chunk, o).start()

        xs = pl.ds(chunk * part, part)
        own = pltpu.make_async_copy(
            back.at[tm, :, xs], ret.at[tm, :, xs], local_sem.at[5 + chunk]
        )
        own.start()
        own_back.append(own)

    out_upd = []
    planes = 2 * part
    for chunk in range(CHUNKS):
        own_back[chunk].wait()
        xs = pl.ds(chunk * part, part)

        @pl.loop(1, ROWS)
        def _(o):
            peer = jnp.bitwise_xor(tm, o)
            landing = ret.at[peer, :, xs]
            remote(
                landing, landing, back_send.at[chunk, o], back_recv.at[chunk, o], (peer, sp)
            ).wait_recv()

        for at in range(planes):
            step, x = at // part, chunk * part + at % part
            for pair in range(NY // (2 * SUB)):
                tiles = [
                    jnp.concatenate([ret[4 * pair + 2 * i, step, x], ret[4 * pair + 2 * i + 1, step, x]], axis=1)
                    for i in (0, 1)
                ]
                high, low = split(jnp.concatenate(tiles, axis=0))
                rows = pl.ds(at * NY + pair * 2 * SUB, 2 * SUB)
                row_hi[rows] = high
                row_lo[rows] = low
        high, low = row_hi[pl.ds(0, planes * NY)], row_lo[pl.ds(0, planes * NY)]
        value = dot(high, zb[0]) + dot(low, zb[0]) + dot(high, zb[1])
        for at in range(planes):
            step, x = at // part, chunk * part + at % part
            scale = jnp.exp(
                jnp.full(
                    (SUB, LANE),
                    (2 * tm + step).astype(jnp.float32) * (-math.log(alpha_value) / STEPS) - math.log(STEPS),
                )
            )
            delta = along_y(1, value[at * NY : (at + 1) * NY])
            upd[step, x] = st[step, x + 1] + delta * jnp.tile(scale, (NY // SUB, NZ // LANE))
        copy = pltpu.make_async_copy(upd.at[:, xs], updated.at[:, xs], local_sem.at[7 + chunk])
        copy.start()
        out_upd.append(copy)

    for copy in edges:
        copy.wait_send()

    @pl.when(tm < ROWS - 1)
    def _():
        slab.wait_send()

    for step in (1, 0):
        for copy in halo_copies(step):
            copy.wait_send()

    @pl.loop(1, ROWS)
    def _(o):
        for step in (1, 0):
            fore_copy(step, o)[1].wait_send()
        for chunk in range(CHUNKS):
            back_copy(chunk, o).wait_send()

    out_res.wait()
    for copy in out_upd:
        copy.wait()


def body(state, initial):
    mu, zf, zb, ymat, table = (jnp.asarray(c) for c in constants())
    whole = jax.ShapeDtypeStruct(state.shape, jnp.float32)
    steps = STEPS // ROWS
    vmem = pl.BlockSpec(memory_space=pltpu.VMEM)
    anywhere = pl.BlockSpec(memory_space=pl.ANY)
    f32 = jnp.float32
    return pl.pallas_call(
        kernel,
        out_shape=(whole, whole),
        in_specs=[anywhere, anywhere, vmem, vmem, vmem, vmem, pl.BlockSpec(memory_space=pltpu.SMEM)],
        out_specs=(anywhere, anywhere),
        scratch_shapes=[
            pltpu.VMEM((steps, SLAB + 2, NY, NZ), f32),
            pltpu.VMEM((SLAB, NY, NZ), f32),
            pltpu.VMEM((steps, SLAB, NY, NZ), f32),
            pltpu.VMEM((steps, SLAB, NY, NZ), f32),
            pltpu.VMEM((ROWS, steps, SLAB, SUB, LANE), f32),
            pltpu.VMEM((steps, ROWS, WIDE, SUB, LANE), f32),
            pltpu.VMEM((STEPS, WIDE, SUB, LANE), f32),
            pltpu.VMEM((ROWS, steps, SLAB, SUB, LANE), f32),
            pltpu.VMEM((ROWS, steps, SLAB, SUB, LANE), f32),
            pltpu.VMEM((SLAB * NY, NZ), jnp.bfloat16),
            pltpu.VMEM((SLAB * NY, NZ), jnp.bfloat16),
            pltpu.SemaphoreType.DMA((7 + CHUNKS,)),
            pltpu.SemaphoreType.DMA((2,)),
            pltpu.SemaphoreType.DMA((2,)),
            pltpu.SemaphoreType.DMA((1,)),
            pltpu.SemaphoreType.DMA((1,)),
            pltpu.SemaphoreType.DMA((steps, ROWS)),
            pltpu.SemaphoreType.DMA((steps, ROWS)),
            pltpu.SemaphoreType.DMA((steps, 2)),
            pltpu.SemaphoreType.DMA((steps, 2)),
            pltpu.SemaphoreType.DMA((CHUNKS, ROWS)),
            pltpu.SemaphoreType.DMA((CHUNKS, ROWS)),
        ],
        compiler_params=pltpu.CompilerParams(
            collective_id=0, has_side_effects=True, vmem_limit_bytes=40 * 2**20
        ),
        cost_estimate=pl.CostEstimate(flops=10**9, bytes_accessed=8 * 2**20, transcendentals=0),
    )(state, initial, mu, zf, zb, ymat, table)


def solution(mesh):
    in_specs = (P("tm", "space", None, None), P("space", None, None))
    out_specs = (P("tm", "space", None, None), P("tm", "space", None, None))
    return jax.shard_map(body, mesh=mesh, in_specs=in_specs, out_specs=out_specs, check_vma=False)
```

```python
import math

import jax
import jax.numpy as jnp
import ml_dtypes
import numpy as np
from jax import lax
from jax.experimental import pallas as pl
from jax.experimental.pallas import tpu as pltpu
from jax.sharding import PartitionSpec as P

MESH = pl.DeviceIdType.MESH
SWEEPS = 6
STEPS, NX, NY, NZ = 32, 128, 64, 256
ROWS = 16
RING = 16
PAIR, DEPTH = 2, 8
GROUP = ROWS * PAIR
SLAB = NX // RING
REACH = SWEEPS - 1
WIDE = SLAB + 2 * REACH
SUB, LANE = 8, 128
HALF = SUB // PAIR
GAMMA = (STEPS // 2 - 1) * 2 * SWEEPS
CHUNKS = 2

alpha_value = 0.1
time_step = 0.1
couple_first = 0.4
couple_cross = 0.05
reaction_shift = 0.1
relaxation = 0.9
rho = alpha_value ** (1.0 / STEPS)


def real_basis(n):
    cells = np.arange(n)
    rows, freq = np.zeros((n, n)), np.zeros(n)
    rows[0] = 1.0 / math.sqrt(n)
    rows[1] = (-1.0) ** cells / math.sqrt(n)
    freq[1] = n // 2
    for k in range(1, n // 2):
        angle = 2.0 * math.pi * (k * cells % n) / n
        rows[2 * k] = math.sqrt(2.0 / n) * np.cos(angle)
        rows[2 * k + 1] = math.sqrt(2.0 / n) * np.sin(angle)
        freq[2 * k] = freq[2 * k + 1] = k
    return rows, freq


def halves(matrix):
    high = matrix.astype(ml_dtypes.bfloat16)
    low = (matrix - high.astype(np.float64)).astype(ml_dtypes.bfloat16)
    return high, low


def mode_factors(k):
    theta = 2.0 * math.pi * k / STEPS
    diag = 1.0 + reaction_shift + 2.0 * couple_first + 4.0 * couple_cross
    shift = complex(diag - rho * math.cos(theta), rho * math.sin(theta))
    scale = relaxation / shift
    beta = couple_first * scale
    roots = [complex(np.exp(2j * math.pi * j / SWEEPS)) for j in range(1, SWEEPS)]
    return [(1.0 - relaxation - root) / beta for root in roots], beta**REACH * scale


def constants():
    basis_z, freq_z = real_basis(NZ)
    basis_y, freq_y = real_basis(NY)
    wave_z = 2.0 * np.cos(2.0 * math.pi * freq_z / NZ)
    wave_y = 2.0 * np.cos(2.0 * math.pi * freq_y / NY)
    mu = (couple_cross / couple_first) * (wave_y[:, None] + wave_z[None, :])
    mu = mu.reshape(ROWS, HALF, PAIR, LANE).transpose(0, 2, 1, 3)
    mu = np.tile(mu.reshape(GROUP, HALF, LANE), (1, PAIR, 1)).astype(np.float32)
    zf = np.stack(halves(basis_z.T))
    zb = np.stack(halves(basis_z))
    yh, yl = halves(basis_y)
    yf = np.concatenate([yh, yh, yl], axis=1)
    yh, yl = halves(basis_y.T)
    yb = np.concatenate([yh, yh, yl], axis=1)
    table = []
    for k in range(1, STEPS // 2):
        factors, last = mode_factors(k)
        for value in factors + [last]:
            table += [value.real, value.imag]
    gamma = alpha_value ** (np.arange(STEPS) / STEPS)
    table += list(gamma) + list(1.0 / (STEPS * gamma))
    return mu, zf, zb, np.stack([yf, yb]), np.asarray(table, np.float32)


def split(value):
    high = value.astype(jnp.bfloat16)
    low = (value - high.astype(jnp.float32)).astype(jnp.bfloat16)
    return high, low


def dot(a, b):
    return jnp.dot(a, b, preferred_element_type=jnp.float32)


def rfft(x):
    n = len(x)
    if n == 2:
        return [(x[0] + x[1], None), (x[0] - x[1], None)]
    even, odd = rfft(x[0::2]), rfft(x[1::2])
    h, q = n // 2, n // 4
    out = [None] * (h + 1)
    out[0] = (even[0][0] + odd[0][0], None)
    out[h] = (even[0][0] - odd[0][0], None)
    out[q] = (even[q][0], -odd[q][0])
    for k in range(1, q):
        c, s = math.cos(2.0 * math.pi * k / n), -math.sin(2.0 * math.pi * k / n)
        er, ei = even[k]
        pr, pi = odd[k]
        tr, ti = c * pr - s * pi, c * pi + s * pr
        out[k] = (er + tr, ei + ti)
        out[h - k] = (er - tr, ti - ei)
    return out


def irfft(modes):
    n = 2 * (len(modes) - 1)
    if n == 2:
        return [modes[0][0] + modes[1][0], modes[0][0] - modes[1][0]]
    h, q = n // 2, n // 4
    even, odd = [None] * (q + 1), [None] * (q + 1)
    even[0] = (modes[0][0] + modes[h][0], None)
    odd[0] = (modes[0][0] - modes[h][0], None)
    even[q] = (2.0 * modes[q][0], None)
    odd[q] = (-2.0 * modes[q][1], None)
    for k in range(1, q):
        c, s = math.cos(2.0 * math.pi * k / n), math.sin(2.0 * math.pi * k / n)
        ar, ai = modes[k]
        br, bi = modes[h - k]
        even[k] = (ar + br, ai - bi)
        dr, di = ar - br, ai + bi
        odd[k] = (c * dr - s * di, c * di + s * dr)
    out = [None] * n
    out[0::2], out[1::2] = irfft(even), irfft(odd)
    return out


def kernel(
    state, initial, mu_all, zf_all, zb_all, ymat_all, table_all,
    updated, residual,
    st, bef, res, upd, fore, mid, spec, back, ret, row_hi, row_lo, mu_ref, zf, zb, ymat, table,
    local_sem, edge_send, edge_recv, slab_send, slab_recv,
    fore_send, fore_recv, halo_send, halo_recv, back_send, back_recv,
):
    tm, sp = lax.axis_index("tm"), lax.axis_index("space")
    pair, z = sp // DEPTH, lax.rem(sp, DEPTH)
    up, down = lax.rem(sp + 1, RING), lax.rem(sp + RING - 1, RING)
    above = pair * DEPTH + lax.rem(z + 1, DEPTH)
    below = pair * DEPTH + lax.rem(z + DEPTH - 1, DEPTH)

    def remote(src, dst, send, recv, device):
        return pltpu.make_async_remote_copy(
            src_ref=src, dst_ref=dst, send_sem=send, recv_sem=recv,
            device_id=device, device_id_type=MESH,
        )

    def member(o):
        t, p = jnp.bitwise_xor(tm, lax.rem(o, ROWS)), lax.rem(pair + o // ROWS, PAIR)
        return t, p, (t, p * DEPTH + z)

    barrier = pltpu.get_barrier_semaphore()
    for near in (up, down, above, below):
        pl.semaphore_signal(barrier, inc=1, device_id=(tm, near), device_id_type=MESH)

    @pl.loop(1, GROUP)
    def _(o):
        pl.semaphore_signal(barrier, inc=1, device_id=member(o)[2], device_id_type=MESH)

    load = pltpu.make_async_copy(state, st.at[:, pl.ds(1, SLAB)], local_sem.at[0])
    load.start()
    loads = [
        pltpu.make_async_copy(src, dst, local_sem.at[7 + 2 * CHUNKS + i])
        for i, (src, dst) in enumerate(
            ((ymat_all, ymat), (zf_all, zf), (table_all, table), (mu_all, mu_ref), (zb_all, zb))
        )
    ]
    for copy in loads:
        copy.start()

    @pl.when(tm == 0)
    def _():
        first = pltpu.make_async_copy(initial, bef, local_sem.at[1])
        first.start()
        first.wait()

    load.wait()
    for copy in loads:
        copy.wait()
    pl.semaphore_wait(barrier, GROUP + 3)

    edges = [
        remote(st.at[:, SLAB], st.at[:, 0], edge_send.at[0], edge_recv.at[0], (tm, up)),
        remote(st.at[:, 1], st.at[:, SLAB + 1], edge_send.at[1], edge_recv.at[1], (tm, down)),
    ]
    for copy in edges:
        copy.start()
    slab = remote(
        st.at[1, pl.ds(1, SLAB)], bef, slab_send.at[0], slab_recv.at[0],
        (lax.rem(tm + 1, ROWS), sp),
    )

    @pl.when(tm < ROWS - 1)
    def _():
        slab.start()

    def own_part(step, x):
        s = st[step, x + 1]
        near = st[step, x] + st[step, x + 2]
        cross = (
            pltpu.roll(s, 1, 0) + pltpu.roll(s, NY - 1, 0)
            + pltpu.roll(s, 1, 1) + pltpu.roll(s, NZ - 1, 1)
        )
        laplace = couple_first * (near - 2.0 * s) + couple_cross * (cross - 4.0 * s)
        return laplace - s + time_step * (s - s * s * s)

    def along_y(which, value):
        high, low = split(value)
        return dot(ymat[which], jnp.concatenate([high, low, high], axis=0))

    def keep_rows(at, value):
        high, low = split(value)
        rows = pl.ds(pl.multiple_of(at * NY, NY), NY)
        row_hi[rows] = high
        row_lo[rows] = low

    def along_z(matrix):
        high = row_hi[...]
        return dot(high, matrix[0]) + dot(row_lo[...], matrix[0]) + dot(high, matrix[1])

    def transform(step):
        gamma = table[GAMMA + 2 * tm + step]
        rows = along_z(zf)
        for x in range(SLAB):
            for g in range(GROUP):
                r0, c0 = x * NY + (g // PAIR) * HALF, (g % PAIR) * LANE
                fore[g, step, x] = rows[r0 : r0 + HALF, c0 : c0 + LANE] * gamma

    def landing_fore(step, t, p):
        return mid.at[step, t, pl.ds(REACH, SLAB), pl.ds(pl.multiple_of(HALF * p, HALF), HALF)]

    def fore_copy(step, o):
        t, p, device = member(o)
        return remote(
            fore.at[t * PAIR + p, step], landing_fore(step, tm, pair),
            fore_send.at[step, o], fore_recv.at[step, o], device,
        )

    def send_fore(step):
        @pl.loop(1, GROUP)
        def _(o):
            fore_copy(step, o).start()

        own = pltpu.make_async_copy(
            fore.at[tm * PAIR + pair, step], landing_fore(step, tm, pair), local_sem.at[2 + step]
        )
        own.start()
        return own

    @pl.loop(1, SLAB - 1)
    def _(x):
        value = own_part(1, x) + st[0, x + 1]
        res[1, x] = value
        keep_rows(x, along_y(0, value))

    for copy in edges:
        copy.wait_recv()
    for x in (0, SLAB - 1):
        value = own_part(1, x) + st[0, x + 1]
        res[1, x] = value
        keep_rows(x, along_y(0, value))
    transform(1)
    own_odd = send_fore(1)

    @pl.loop(0, SLAB)
    def _(x):
        res[0, x] = own_part(0, x)

    @pl.when(tm > 0)
    def _():
        slab.wait_recv()

    @pl.loop(0, SLAB)
    def _(x):
        value = res[0, x] + bef[x]
        res[0, x] = value
        keep_rows(x, along_y(0, value))

    transform(0)
    own_even = send_fore(0)
    out_res = pltpu.make_async_copy(res, residual, local_sem.at[4])
    out_res.start()

    def halo_copies(step):
        return [
            remote(
                mid.at[step, :, pl.ds(SLAB, REACH)], mid.at[step, :, pl.ds(0, REACH)],
                halo_send.at[step, 0], halo_recv.at[step, 0], (tm, above),
            ),
            remote(
                mid.at[step, :, pl.ds(REACH, REACH)], mid.at[step, :, pl.ds(REACH + SLAB, REACH)],
                halo_send.at[step, 1], halo_recv.at[step, 1], (tm, below),
            ),
        ]

    for step, own in ((1, own_odd), (0, own_even)):
        own.wait()

        @pl.loop(1, GROUP)
        def _(o):
            t, p, device = member(o)
            landing = landing_fore(step, t, p)
            remote(
                landing, landing, fore_send.at[step, o], fore_recv.at[step, o], device
            ).wait_recv()

        for copy in halo_copies(step):
            copy.start()

    def to_modes(x, turned=None):
        values = [mid[n % 2, n // 2, x] for n in range(STEPS)]
        modes = rfft(values)
        slots = [modes[0][0], modes[STEPS // 2][0]]
        for k in range(1, STEPS // 2):
            slots += [modes[k][0], modes[k][1]]
        for slot, value in enumerate(slots):
            if turned is not None:
                value = jnp.where(turned, pltpu.roll(value, HALF, 0), value)
            spec[slot, x] = value

    @pl.loop(REACH, REACH + SLAB)
    def _(x):
        to_modes(x)

    for step in (1, 0):
        for copy in halo_copies(step):
            copy.wait_recv()

    @pl.loop(0, REACH)
    def _(x):
        to_modes(x, z == 0)

    @pl.loop(REACH + SLAB, WIDE)
    def _(x):
        to_modes(x, z == DEPTH - 1)

    mu = mu_ref[tm * PAIR + pair]

    for slot, k in ((0, 0), (1, STEPS // 2)):
        factors, last = mode_factors(k)
        v = [spec[slot, x] for x in range(WIDE)]
        for j in (0, 1):
            dr, square = mu + factors[j].real, factors[j].imag ** 2
            first = [v[x - 1] + v[x + 1] + dr * v[x] for x in range(1, len(v) - 1)]
            v = [
                first[x - 1] + first[x + 1] + dr * first[x] + square * v[x + 1]
                for x in range(1, len(first) - 1)
            ]
        dr = mu + factors[2].real
        v = [v[x - 1] + v[x + 1] + dr * v[x] for x in range(1, len(v) - 1)]
        for x in range(SLAB):
            spec[slot, x] = last.real * v[x]

    @pl.loop(1, STEPS // 2)
    def _(k):
        base = (k - 1) * 2 * SWEEPS
        vr = [spec[2 * k, x] for x in range(WIDE)]
        vi = [spec[2 * k + 1, x] for x in range(WIDE)]
        for j in range(REACH):
            dr, di = mu + table[base + 2 * j], table[base + 2 * j + 1]
            inner = range(1, len(vr) - 1)
            vr, vi = (
                [vr[x - 1] + vr[x + 1] + dr * vr[x] - di * vi[x] for x in inner],
                [vi[x - 1] + vi[x + 1] + dr * vi[x] + di * vr[x] for x in inner],
            )
        lr, li = table[base + 2 * REACH], table[base + 2 * REACH + 1]
        for x in range(SLAB):
            spec[2 * k, x] = lr * vr[x] - li * vi[x]
            spec[2 * k + 1, x] = lr * vi[x] + li * vr[x]

    part = SLAB // CHUNKS

    def leaving(chunk, t, p):
        xs = pl.ds(chunk * part, part)
        return back.at[t, :, xs, pl.ds(pl.multiple_of(HALF * p, HALF), HALF)]

    def back_copy(chunk, o):
        t, p, device = member(o)
        return remote(
            leaving(chunk, t, p), ret.at[tm * PAIR + pair, :, pl.ds(chunk * part, part)],
            back_send.at[chunk, o], back_recv.at[chunk, o], device,
        )

    own_back = []
    for chunk in range(CHUNKS):
        @pl.loop(chunk * part, (chunk + 1) * part)
        def _(x):
            modes = [(spec[0, x], None)]
            modes += [(spec[2 * k, x], spec[2 * k + 1, x]) for k in range(1, STEPS // 2)]
            modes += [(spec[1, x], None)]
            values = irfft(modes)
            for n in range(STEPS):
                back[n // 2, n % 2, x] = values[n]

        @pl.loop(1, GROUP)
        def _(o):
            back_copy(chunk, o).start()

        own = pltpu.make_async_copy(
            leaving(chunk, tm, pair), ret.at[tm * PAIR + pair, :, pl.ds(chunk * part, part)],
            local_sem.at[7 + chunk],
        )
        own.start()
        own_back.append(own)

    out_upd = []
    planes = 2 * part
    for chunk in range(CHUNKS):
        own_back[chunk].wait()
        xs = pl.ds(chunk * part, part)

        @pl.loop(1, GROUP)
        def _(o):
            t, p, device = member(o)
            landing = ret.at[t * PAIR + p, :, xs]
            remote(
                landing, landing, back_send.at[chunk, o], back_recv.at[chunk, o], device
            ).wait_recv()

        for at in range(planes):
            step, x = at // part, chunk * part + at % part
            for four in range(NY // (4 * HALF)):
                tiles = [
                    jnp.concatenate(
                        [ret[(4 * four + i) * PAIR + p, step, x] for p in range(PAIR)], axis=1
                    )
                    for i in range(4)
                ]
                high, low = split(jnp.concatenate(tiles, axis=0))
                rows = pl.ds(at * NY + four * 4 * HALF, 4 * HALF)
                row_hi[rows] = high
                row_lo[rows] = low
        high, low = row_hi[pl.ds(0, planes * NY)], row_lo[pl.ds(0, planes * NY)]
        value = dot(high, zb[0]) + dot(low, zb[0]) + dot(high, zb[1])
        for at in range(planes):
            step, x = at // part, chunk * part + at % part
            delta = along_y(1, value[at * NY : (at + 1) * NY])
            upd[step, x] = st[step, x + 1] + table[GAMMA + STEPS + 2 * tm + step] * delta
        copy = pltpu.make_async_copy(
            upd.at[:, xs], updated.at[:, xs], local_sem.at[7 + CHUNKS + chunk]
        )
        copy.start()
        out_upd.append(copy)

    for copy in edges:
        copy.wait_send()

    @pl.when(tm < ROWS - 1)
    def _():
        slab.wait_send()

    for step in (1, 0):
        for copy in halo_copies(step):
            copy.wait_send()

    @pl.loop(1, GROUP)
    def _(o):
        for step in (1, 0):
            fore_copy(step, o).wait_send()
        for chunk in range(CHUNKS):
            back_copy(chunk, o).wait_send()

    out_res.wait()
    for copy in out_upd:
        copy.wait()


def body(state, initial):
    mu, zf, zb, ymat, table = (jnp.asarray(c) for c in constants())
    whole = jax.ShapeDtypeStruct(state.shape, jnp.float32)
    steps = STEPS // ROWS
    hbm = pl.BlockSpec(memory_space=pltpu.HBM)
    f32 = jnp.float32
    return pl.pallas_call(
        kernel,
        out_shape=(whole, whole),
        in_specs=[hbm] * 7,
        out_specs=(hbm, hbm),
        scratch_shapes=[
            pltpu.VMEM((steps, SLAB + 2, NY, NZ), f32),
            pltpu.VMEM((SLAB, NY, NZ), f32),
            pltpu.VMEM((steps, SLAB, NY, NZ), f32),
            pltpu.VMEM((steps, SLAB, NY, NZ), f32),
            pltpu.VMEM((GROUP, steps, SLAB, HALF, LANE), f32),
            pltpu.VMEM((steps, ROWS, WIDE, SUB, LANE), f32),
            pltpu.VMEM((STEPS, WIDE, SUB, LANE), f32),
            pltpu.VMEM((ROWS, steps, SLAB, SUB, LANE), f32),
            pltpu.VMEM((GROUP, steps, SLAB, HALF, LANE), f32),
            pltpu.VMEM((SLAB * NY, NZ), jnp.bfloat16),
            pltpu.VMEM((SLAB * NY, NZ), jnp.bfloat16),
            pltpu.VMEM(mu.shape, f32),
            pltpu.VMEM(zf.shape, jnp.bfloat16),
            pltpu.VMEM(zb.shape, jnp.bfloat16),
            pltpu.VMEM(ymat.shape, jnp.bfloat16),
            pltpu.SMEM(table.shape, f32),
            pltpu.SemaphoreType.DMA((12 + 2 * CHUNKS,)),
            pltpu.SemaphoreType.DMA((2,)),
            pltpu.SemaphoreType.DMA((2,)),
            pltpu.SemaphoreType.DMA((1,)),
            pltpu.SemaphoreType.DMA((1,)),
            pltpu.SemaphoreType.DMA((steps, GROUP)),
            pltpu.SemaphoreType.DMA((steps, GROUP)),
            pltpu.SemaphoreType.DMA((steps, 2)),
            pltpu.SemaphoreType.DMA((steps, 2)),
            pltpu.SemaphoreType.DMA((CHUNKS, GROUP)),
            pltpu.SemaphoreType.DMA((CHUNKS, GROUP)),
        ],
        compiler_params=pltpu.CompilerParams(
            collective_id=0, has_side_effects=True, vmem_limit_bytes=60 * 2**20
        ),
        cost_estimate=pl.CostEstimate(flops=10**9, bytes_accessed=8 * 2**20, transcendentals=0),
    )(state, initial, mu, zf, zb, ymat, table)


def solution(mesh):
    in_specs = (P("tm", "space", None, None), P("space", None, None))
    out_specs = (P("tm", "space", None, None), P("tm", "space", None, None))
    return jax.shard_map(body, mesh=mesh, in_specs=in_specs, out_specs=out_specs, check_vma=False)
```

```python
import math

import jax
import jax.numpy as jnp
import ml_dtypes
import numpy as np
from jax import lax
from jax.experimental import pallas as pl
from jax.experimental.pallas import tpu as pltpu
from jax.sharding import PartitionSpec as P

MESH = pl.DeviceIdType.MESH
SWEEPS = 6
STEPS, NX, NY, NZ = 32, 128, 64, 256
ROWS = 16
RING = 16
PAIR, DEPTH = 2, 8
GROUP = ROWS * PAIR
SLAB = NX // RING
REACH = SWEEPS - 1
WIDE = SLAB + 2 * REACH
SUB, LANE = 8, 128
HALF = SUB // PAIR
REAL = (STEPS // 2 - 1) * 2 * SWEEPS
GAMMA = REAL + 2 * SWEEPS
CHUNKS = 2
OWN = SLAB // 2
BATCH = 2 * PAIR

alpha_value = 0.1
time_step = 0.1
couple_first = 0.4
couple_cross = 0.05
reaction_shift = 0.1
relaxation = 0.9
rho = alpha_value ** (1.0 / STEPS)


def real_basis(n):
    cells = np.arange(n)
    rows, freq = np.zeros((n, n)), np.zeros(n)
    rows[0] = 1.0 / math.sqrt(n)
    rows[1] = (-1.0) ** cells / math.sqrt(n)
    freq[1] = n // 2
    for k in range(1, n // 2):
        angle = 2.0 * math.pi * (k * cells % n) / n
        rows[2 * k] = math.sqrt(2.0 / n) * np.cos(angle)
        rows[2 * k + 1] = math.sqrt(2.0 / n) * np.sin(angle)
        freq[2 * k] = freq[2 * k + 1] = k
    return rows, freq


def halves(matrix):
    high = matrix.astype(ml_dtypes.bfloat16)
    low = (matrix - high.astype(np.float64)).astype(ml_dtypes.bfloat16)
    return high, low


def mode_factors(k):
    theta = 2.0 * math.pi * k / STEPS
    diag = 1.0 + reaction_shift + 2.0 * couple_first + 4.0 * couple_cross
    shift = complex(diag - rho * math.cos(theta), rho * math.sin(theta))
    scale = relaxation / shift
    beta = couple_first * scale
    roots = [complex(np.exp(2j * math.pi * j / SWEEPS)) for j in range(1, SWEEPS)]
    return [(1.0 - relaxation - root) / beta for root in roots], beta**REACH * scale


def constants():
    basis_z, freq_z = real_basis(NZ)
    basis_y, freq_y = real_basis(NY)
    wave_z = 2.0 * np.cos(2.0 * math.pi * freq_z / NZ)
    wave_y = 2.0 * np.cos(2.0 * math.pi * freq_y / NY)
    mu = (couple_cross / couple_first) * (wave_y[:, None] + wave_z[None, :])
    mu = mu.reshape(ROWS, HALF, PAIR, LANE).transpose(0, 2, 1, 3)
    mu = np.tile(mu.reshape(GROUP, HALF, LANE), (1, PAIR, 1)).astype(np.float32)
    zf = np.stack(halves(basis_z.T))
    zb = np.stack(halves(basis_z))
    yh, yl = halves(basis_y)
    yf = np.concatenate([yh, yh, yl], axis=1)
    yh, yl = halves(basis_y.T)
    yb = np.concatenate([yh, yh, yl], axis=1)
    table = []
    for k in range(1, STEPS // 2):
        factors, last = mode_factors(k)
        for value in factors + [last]:
            table += [value.real, value.imag]
    for k in (0, STEPS // 2):
        factors, last = mode_factors(k)
        for value in factors[:2]:
            table += [value.real, value.imag**2]
        table += [factors[2].real, last.real]
    gamma = alpha_value ** (np.arange(STEPS) / STEPS)
    table += list(gamma) + list(1.0 / (STEPS * gamma))
    return mu, zf, zb, np.stack([yf, yb]), np.asarray(table, np.float32)


def split(value):
    high = value.astype(jnp.bfloat16)
    low = (value - high.astype(jnp.float32)).astype(jnp.bfloat16)
    return high, low


def dot(a, b):
    return jnp.dot(a, b, preferred_element_type=jnp.float32)


def rfft(x):
    n = len(x)
    if n == 2:
        return [(x[0] + x[1], None), (x[0] - x[1], None)]
    even, odd = rfft(x[0::2]), rfft(x[1::2])
    h, q = n // 2, n // 4
    out = [None] * (h + 1)
    out[0] = (even[0][0] + odd[0][0], None)
    out[h] = (even[0][0] - odd[0][0], None)
    out[q] = (even[q][0], -odd[q][0])
    for k in range(1, q):
        c, s = math.cos(2.0 * math.pi * k / n), -math.sin(2.0 * math.pi * k / n)
        er, ei = even[k]
        pr, pi = odd[k]
        tr, ti = c * pr - s * pi, c * pi + s * pr
        out[k] = (er + tr, ei + ti)
        out[h - k] = (er - tr, ti - ei)
    return out


def irfft(modes):
    n = 2 * (len(modes) - 1)
    if n == 2:
        return [modes[0][0] + modes[1][0], modes[0][0] - modes[1][0]]
    h, q = n // 2, n // 4
    even, odd = [None] * (q + 1), [None] * (q + 1)
    even[0] = (modes[0][0] + modes[h][0], None)
    odd[0] = (modes[0][0] - modes[h][0], None)
    even[q] = (2.0 * modes[q][0], None)
    odd[q] = (-2.0 * modes[q][1], None)
    for k in range(1, q):
        c, s = math.cos(2.0 * math.pi * k / n), math.sin(2.0 * math.pi * k / n)
        ar, ai = modes[k]
        br, bi = modes[h - k]
        even[k] = (ar + br, ai - bi)
        dr, di = ar - br, ai + bi
        odd[k] = (c * dr - s * di, c * di + s * dr)
    out = [None] * n
    out[0::2], out[1::2] = irfft(even), irfft(odd)
    return out


def kernel(
    state, initial, mu_all, zf_all, zb_all, ymat_all, table_all,
    updated, residual,
    st, late, res, upd, fore, third, mid, mid3, spec, back, ret, mu_ref, zf, zb, ymat, table,
    load_sem, own_sem, out_sem, edge_send, edge_recv, slab_send, slab_recv,
    fore_send, fore_recv, third_send, third_recv, halo_send, halo_recv, back_send, back_recv,
):
    tm, sp = lax.axis_index("tm"), lax.axis_index("space")
    pair, z = sp // DEPTH, lax.rem(sp, DEPTH)
    up, down = lax.rem(sp + 1, RING), lax.rem(sp + RING - 1, RING)
    above = pair * DEPTH + lax.rem(z + 1, DEPTH)
    below = pair * DEPTH + lax.rem(z + DEPTH - 1, DEPTH)
    both = pl.ds(1, 2)

    def remote(src, dst, send, recv, device):
        return pltpu.make_async_remote_copy(
            src_ref=src, dst_ref=dst, send_sem=send, recv_sem=recv,
            device_id=device, device_id_type=MESH,
        )

    def member(o):
        bit = [lax.rem(o // 2**i, 2) for i in range(5)]
        t = jnp.bitwise_xor(tm, bit[0] + 8 * bit[2] + 2 * bit[3] + 4 * bit[4])
        p = lax.rem(pair + bit[1], PAIR)
        return t, p, (t, p * DEPTH + z)

    nears = (up, down, above, below)
    barrier = pltpu.get_barrier_semaphore()
    for near in nears:
        pl.semaphore_signal(barrier, inc=1, device_id=(tm, near), device_id_type=MESH)

    @pl.loop(1, GROUP)
    def _(o):
        pl.semaphore_signal(barrier, inc=1, device_id=member(o)[2], device_id_type=MESH)

    loads = [
        pltpu.make_async_copy(src, dst, load_sem.at[i])
        for i, (src, dst) in enumerate(
            (
                (state, st.at[both, pl.ds(1, SLAB)]), (ymat_all, ymat), (zf_all, zf),
                (table_all, table), (mu_all, mu_ref), (zb_all, zb),
            )
        )
    ]
    for copy in loads:
        copy.start()

    @pl.when(tm == 0)
    def _():
        first = pltpu.make_async_copy(initial, st.at[0, pl.ds(1, SLAB)], own_sem.at[0])
        first.start()
        first.wait()

    odd = lax.rem(tm, 2) == 1
    extra = jnp.logical_and(odd, tm < ROWS - 1)
    later = jnp.logical_and(jnp.logical_not(odd), tm > 0)

    @pl.when(later)
    def _():
        @pl.loop(0, SLAB)
        def _(x):
            st[0, x + 1] = jnp.zeros((NY, NZ), jnp.float32)

    for copy in loads:
        copy.wait()

    edges = [
        remote(st.at[both, SLAB], st.at[both, 0], edge_send.at[0], edge_recv.at[0], (tm, up)),
        remote(st.at[both, 1], st.at[both, SLAB + 1], edge_send.at[1], edge_recv.at[1], (tm, down)),
    ]
    slab, slab_later = (
        remote(
            st.at[2, pl.ds(1, SLAB)], to, slab_send.at[0], slab_recv.at[0],
            (lax.rem(tm + 1, ROWS), sp),
        )
        for to in (st.at[0, pl.ds(1, SLAB)], late)
    )
    pl.semaphore_wait(barrier, GROUP - 1 + len(nears))
    for copy in edges:
        copy.start()

    @pl.when(jnp.logical_not(odd))
    def _():
        slab.start()

    def residual_of(step, x):
        s = st[step + 1, x + 1]
        near = st[step + 1, x] + st[step + 1, x + 2]
        cross = (
            pltpu.roll(s, 1, 0) + pltpu.roll(s, NY - 1, 0)
            + pltpu.roll(s, 1, 1) + pltpu.roll(s, NZ - 1, 1)
        )
        laplace = couple_first * (near - 2.0 * s) + couple_cross * (cross - 4.0 * s)
        return st[step, x + 1] - s + laplace + time_step * (s - s * s * s)

    def along_y(which, value):
        high, low = split(value)
        return dot(ymat[which], jnp.concatenate([high, low, high], axis=0))

    def along_z(matrix, value):
        high, low = split(value)
        return dot(high, matrix[0]) + dot(low, matrix[0]) + dot(high, matrix[1])

    def part_of(p):
        return pl.ds(pl.multiple_of(HALF * p, HALF), HALF)

    own_places = pl.ds(0, SLAB)

    def landing_fore(step, t, p):
        return mid.at[step, t, own_places, part_of(p)]

    def own_fore(step):
        return pltpu.make_async_copy(
            fore.at[tm * PAIR + pair, step], landing_fore(step, tm, pair), own_sem.at[step]
        )

    def landing_third(t, p):
        return mid3.at[t // 2, :, part_of(p)]

    def own_third():
        return pltpu.make_async_copy(
            third.at[tm * PAIR + pair], landing_third(tm, pair), own_sem.at[2 + CHUNKS]
        )

    def lay_out(target, place, rows):
        for j in range(2):
            for g in range(GROUP):
                r0, c0 = j * NY + (g // PAIR) * HALF, (g % PAIR) * LANE
                target(g, place + j, rows[r0 : r0 + HALF, c0 : c0 + LANE])

    def work(step, place):
        rows = []
        for j in range(2):
            x = lax.rem(place + j + 1, SLAB)
            value = residual_of(step, x)
            res[step, x] = value
            rows.append(along_y(0, value))
        rows = along_z(zf, jnp.concatenate(rows, axis=0)) * table[GAMMA + 2 * tm + step]

        def put(g, at, value):
            fore[g, step, at] = value

        lay_out(put, place, rows)

    def work_third(place):
        rows = [along_y(0, st[2, lax.rem(place + j + 1, SLAB) + 1]) for j in range(2)]
        rows = along_z(zf, jnp.concatenate(rows, axis=0)) * table[GAMMA + 2 * tm + 2]

        def put(g, at, value):
            third[g, at] = value

        lay_out(put, place, rows)

    @pl.loop(0, OWN - 1)
    def _(i):
        work(1, 2 * i)

    @pl.when(extra)
    def _():
        @pl.loop(0, OWN)
        def _(i):
            work_third(2 * i)

        @pl.loop(1, GROUP)
        def _(o):
            t, p, device = member(o)
            remote(
                third.at[t * PAIR + p], landing_third(tm, pair),
                third_send.at[0], third_recv.at[tm // 2, pair], device,
            ).start()

        own_third().start()

    for copy in edges:
        copy.wait_recv()

    @pl.loop(OWN - 1, 2 * OWN)
    def _(i):
        step, place = 1 - i // OWN, 2 * lax.rem(i, OWN)

        @pl.when(jnp.logical_and(i == OWN, odd))
        def _():
            slab.wait_recv()

        work(step, place)

        @pl.when(lax.rem(i, OWN) == OWN - 1)
        def _():
            @pl.loop(1, GROUP)
            def _(o):
                t, p, device = member(o)
                remote(
                    fore.at[t * PAIR + p, step], landing_fore(step, tm, pair),
                    fore_send.at[step], fore_recv.at[step, o], device,
                ).start()

            own_fore(step).start()

    def halo_copies(step, times=pl.ds(0, ROWS)):
        return [
            remote(
                mid.at[step, times, pl.ds(at, count)], mid.at[step, times, pl.ds(to, count)],
                halo_send.at[step, way], halo_recv.at[step, way], (tm, near),
            )
            for way, near, at, to, count in (
                (0, above, SLAB - REACH - 1, SLAB, REACH),
                (1, below, 0, SLAB + REACH + 1, REACH - 1),
                (2, below, SLAB - 1, SLAB + REACH, 1),
            )
        ]

    @pl.loop(0, 2 * GROUP // BATCH)
    def _(i):
        step, o0 = 1 - i // (GROUP // BATCH), lax.rem(i, GROUP // BATCH) * BATCH

        @pl.when(o0 == 0)
        def _():
            own_fore(step).wait()

        @pl.loop(0, BATCH)
        def _(j):
            @pl.when(o0 + j > 0)
            def _():
                t, p, device = member(o0 + j)
                landing = landing_fore(step, t, p)
                remote(
                    landing, landing, fore_send.at[step], fore_recv.at[step, o0 + j], device
                ).wait_recv()

        chip = member(o0)[0] // 2

        @pl.when(jnp.logical_and(step == 0, chip > 0))
        def _():
            for p in range(PAIR):
                source = 2 * chip - 1
                own = jnp.logical_and(tm == source, pair == p)

                @pl.when(own)
                def _():
                    own_third().wait()

                @pl.when(jnp.logical_not(own))
                def _():
                    landing = landing_third(source, p)
                    remote(
                        landing, landing, third_send.at[0], third_recv.at[source // 2, p],
                        (source, p * DEPTH + z),
                    ).wait_recv()

            mid[0, 2 * chip, own_places] = mid[0, 2 * chip, own_places] + mid3[chip - 1]

        for copy in halo_copies(step, pl.ds(2 * chip, 2)):
            copy.start()

    @pl.when(extra)
    def _():
        slab_later.start()

    @pl.loop(0, WIDE)
    def _(i):
        @pl.when(i == SLAB)
        def _():
            for step in (1, 0):
                for copy in halo_copies(step):
                    copy.wait_recv()

        before, after = jnp.logical_and(i >= SLAB, i < SLAB + REACH), i >= SLAB + REACH
        x = jnp.where(i < SLAB, REACH + lax.rem(i + 1, SLAB), jnp.where(before, i - SLAB, i))
        turned = jnp.logical_or(
            jnp.logical_and(before, z == 0), jnp.logical_and(after, z == DEPTH - 1)
        )
        modes = rfft([mid[n % 2, n // 2, i] for n in range(STEPS)])
        slots = [modes[0][0], modes[STEPS // 2][0]]
        for k in range(1, STEPS // 2):
            slots += [modes[k][0], modes[k][1]]
        for slot, value in enumerate(slots):
            spec[slot, x] = jnp.where(turned, pltpu.roll(value, HALF, 0), value)

    mu = mu_ref[tm * PAIR + pair]

    @pl.loop(0, 2)
    def _(slot):
        base = REAL + slot * SWEEPS
        v = [spec[slot, x] for x in range(WIDE)]
        for j in (0, 1):
            dr, square = mu + table[base + 2 * j], table[base + 2 * j + 1]
            first = [v[x - 1] + v[x + 1] + dr * v[x] for x in range(1, len(v) - 1)]
            v = [
                first[x - 1] + first[x + 1] + dr * first[x] + square * v[x + 1]
                for x in range(1, len(first) - 1)
            ]
        dr = mu + table[base + 4]
        v = [v[x - 1] + v[x + 1] + dr * v[x] for x in range(1, len(v) - 1)]
        for x in range(SLAB):
            spec[slot, x] = table[base + 5] * v[x]

    @pl.loop(1, STEPS // 2)
    def _(k):
        base = (k - 1) * 2 * SWEEPS
        vr = [spec[2 * k, x] for x in range(WIDE)]
        vi = [spec[2 * k + 1, x] for x in range(WIDE)]
        for j in range(REACH):
            dr, di = mu + table[base + 2 * j], table[base + 2 * j + 1]
            inner = range(1, len(vr) - 1)
            vr, vi = (
                [vr[x - 1] + vr[x + 1] + dr * vr[x] - di * vi[x] for x in inner],
                [vi[x - 1] + vi[x + 1] + dr * vi[x] + di * vr[x] for x in inner],
            )
        lr, li = table[base + 2 * REACH], table[base + 2 * REACH + 1]
        for x in range(SLAB):
            spec[2 * k, x] = lr * vr[x] - li * vi[x]
            spec[2 * k + 1, x] = lr * vi[x] + li * vr[x]

    part = SLAB // CHUNKS

    def planes_of(chunk):
        return pl.ds(pl.multiple_of(chunk * part, part), part)

    def leaving(chunk, t, p):
        return back.at[t, :, planes_of(chunk), part_of(p)]

    def landing_back(chunk, t, p):
        return ret.at[t * PAIR + p, :, planes_of(chunk)]

    def own_back(chunk):
        return pltpu.make_async_copy(
            leaving(chunk, tm, pair), landing_back(chunk, tm, pair), own_sem.at[2 + chunk]
        )

    @pl.loop(0, CHUNKS)
    def _(chunk):
        @pl.loop(0, part)
        def _(i):
            x = chunk * part + i
            modes = [(spec[0, x], None)]
            modes += [(spec[2 * k, x], spec[2 * k + 1, x]) for k in range(1, STEPS // 2)]
            modes += [(spec[1, x], None)]
            values = irfft(modes)
            for n in range(STEPS):
                back[n // 2, n % 2, x] = values[n]

        @pl.loop(1, GROUP)
        def _(o):
            t, p, device = member(o)
            remote(
                leaving(chunk, t, p), landing_back(chunk, tm, pair),
                back_send.at[chunk], back_recv.at[chunk, o], device,
            ).start()

        own_back(chunk).start()

    @pl.when(later)
    def _():
        slab_later.wait_recv()

        @pl.loop(0, SLAB)
        def _(x):
            res[0, x] = res[0, x] + late[x]

    out_res = pltpu.make_async_copy(res, residual, out_sem.at[0])
    out_res.start()

    def out_upd(chunk):
        xs = planes_of(chunk)
        return pltpu.make_async_copy(upd.at[:, xs], updated.at[:, xs], out_sem.at[1 + chunk])

    @pl.loop(0, CHUNKS)
    def _(chunk):
        own_back(chunk).wait()

        @pl.loop(1, GROUP)
        def _(o):
            t, p, device = member(o)
            landing = landing_back(chunk, t, p)
            remote(
                landing, landing, back_send.at[chunk], back_recv.at[chunk, o], device
            ).wait_recv()

        @pl.loop(0, part)
        def _(i):
            step, x0 = i // (part // 2), chunk * part + 2 * lax.rem(i, part // 2)
            rows = []
            for j in range(2):
                for r in range(ROWS):
                    rows.append(
                        jnp.concatenate([ret[r * PAIR + p, step, x0 + j] for p in range(PAIR)], axis=1)
                    )
            value = along_z(zb, jnp.concatenate(rows, axis=0))
            scale = table[GAMMA + STEPS + 2 * tm + step]
            for j in range(2):
                delta = along_y(1, value[j * NY : (j + 1) * NY])
                upd[step, x0 + j] = st[step + 1, x0 + j + 1] + scale * delta

        out_upd(chunk).start()

    for copy in edges:
        copy.wait_send()

    @pl.when(tm < ROWS - 1)
    def _():
        slab.wait_send()

    others = pl.ds(0, GROUP - 1)

    @pl.when(extra)
    def _():
        sent = third.at[others]
        remote(sent, sent, third_send.at[0], third_recv.at[0, 0], (tm, above)).wait_send()

    for step in (1, 0):
        for copy in halo_copies(step):
            copy.wait_send()
        sent = fore.at[others, step]
        remote(sent, sent, fore_send.at[step], fore_recv.at[step, 0], (tm, above)).wait_send()
    for chunk in range(CHUNKS):
        sent = ret.at[others, :, planes_of(chunk)]
        remote(sent, sent, back_send.at[chunk], back_recv.at[chunk, 0], (tm, above)).wait_send()
        out_upd(chunk).wait()
    out_res.wait()


def body(state, initial):
    mu, zf, zb, ymat, table = (jnp.asarray(c) for c in constants())
    whole = jax.ShapeDtypeStruct(state.shape, jnp.float32)
    steps = STEPS // ROWS
    hbm = pl.BlockSpec(memory_space=pltpu.HBM)
    f32 = jnp.float32
    return pl.pallas_call(
        kernel,
        out_shape=(whole, whole),
        in_specs=[hbm] * 7,
        out_specs=(hbm, hbm),
        scratch_shapes=[
            pltpu.VMEM((steps + 1, SLAB + 2, NY, NZ), f32),
            pltpu.VMEM((SLAB, NY, NZ), f32),
            pltpu.VMEM((steps, SLAB, NY, NZ), f32),
            pltpu.VMEM((steps, SLAB, NY, NZ), f32),
            pltpu.VMEM((GROUP, steps, SLAB, HALF, LANE), f32),
            pltpu.VMEM((GROUP, SLAB, HALF, LANE), f32),
            pltpu.VMEM((steps, ROWS, WIDE, SUB, LANE), f32),
            pltpu.VMEM((ROWS // 2, SLAB, SUB, LANE), f32),
            pltpu.VMEM((STEPS, WIDE, SUB, LANE), f32),
            pltpu.VMEM((ROWS, steps, SLAB, SUB, LANE), f32),
            pltpu.VMEM((GROUP, steps, SLAB, HALF, LANE), f32),
            pltpu.VMEM(mu.shape, f32),
            pltpu.VMEM(zf.shape, jnp.bfloat16),
            pltpu.VMEM(zb.shape, jnp.bfloat16),
            pltpu.VMEM(ymat.shape, jnp.bfloat16),
            pltpu.SMEM(table.shape, f32),
            pltpu.SemaphoreType.DMA((6,)),
            pltpu.SemaphoreType.DMA((3 + CHUNKS,)),
            pltpu.SemaphoreType.DMA((1 + CHUNKS,)),
            pltpu.SemaphoreType.DMA((2,)),
            pltpu.SemaphoreType.DMA((2,)),
            pltpu.SemaphoreType.DMA((1,)),
            pltpu.SemaphoreType.DMA((1,)),
            pltpu.SemaphoreType.DMA((steps,)),
            pltpu.SemaphoreType.DMA((steps, GROUP)),
            pltpu.SemaphoreType.DMA((1,)),
            pltpu.SemaphoreType.DMA((ROWS // 2, PAIR)),
            pltpu.SemaphoreType.DMA((steps, 3)),
            pltpu.SemaphoreType.DMA((steps, 3)),
            pltpu.SemaphoreType.DMA((CHUNKS,)),
            pltpu.SemaphoreType.DMA((CHUNKS, GROUP)),
        ],
        compiler_params=pltpu.CompilerParams(
            collective_id=0, has_side_effects=True, vmem_limit_bytes=60 * 2**20
        ),
        cost_estimate=pl.CostEstimate(flops=10**9, bytes_accessed=8 * 2**20, transcendentals=0),
    )(state, initial, mu, zf, zb, ymat, table)


def solution(mesh):
    in_specs = (P("tm", "space", None, None), P("space", None, None))
    out_specs = (P("tm", "space", None, None), P("tm", "space", None, None))
    return jax.shard_map(body, mesh=mesh, in_specs=in_specs, out_specs=out_specs, check_vma=False)
```

```python
import math

import jax
import jax.numpy as jnp
import ml_dtypes
import numpy as np
from jax import lax
from jax.experimental import pallas as pl
from jax.experimental.pallas import tpu as pltpu
from jax.sharding import PartitionSpec as P

MESH = pl.DeviceIdType.MESH
SWEEPS = 6
STEPS, NX, NY, NZ = 32, 128, 64, 256
ROWS = 16
RING = 16
PAIR, DEPTH = 2, 8
GROUP = ROWS * PAIR
SLAB = NX // RING
REACH = SWEEPS - 1
WIDE = SLAB + 2 * REACH
SUB, LANE = 8, 128
HALF = SUB // PAIR
REAL = (STEPS // 2 - 1) * 2 * SWEEPS
GAMMA = REAL + 2 * SWEEPS
CHUNKS = 2
OWN = SLAB // 2
PHASES = ((1, 1, 0, SLAB - 2), (0, 1, 0, SLAB - 2), (0, 2, SLAB - 2, 2))
BATCH = 2 * PAIR

alpha_value = 0.1
time_step = 0.1
couple_first = 0.4
couple_cross = 0.05
reaction_shift = 0.1
relaxation = 0.9
rho = alpha_value ** (1.0 / STEPS)


def real_basis(n):
    cells = np.arange(n)
    rows, freq = np.zeros((n, n)), np.zeros(n)
    rows[0] = 1.0 / math.sqrt(n)
    rows[1] = (-1.0) ** cells / math.sqrt(n)
    freq[1] = n // 2
    for k in range(1, n // 2):
        angle = 2.0 * math.pi * (k * cells % n) / n
        rows[2 * k] = math.sqrt(2.0 / n) * np.cos(angle)
        rows[2 * k + 1] = math.sqrt(2.0 / n) * np.sin(angle)
        freq[2 * k] = freq[2 * k + 1] = k
    return rows, freq


def halves(matrix):
    high = matrix.astype(ml_dtypes.bfloat16)
    low = (matrix - high.astype(np.float64)).astype(ml_dtypes.bfloat16)
    return high, low


def mode_factors(k):
    theta = 2.0 * math.pi * k / STEPS
    diag = 1.0 + reaction_shift + 2.0 * couple_first + 4.0 * couple_cross
    shift = complex(diag - rho * math.cos(theta), rho * math.sin(theta))
    scale = relaxation / shift
    beta = couple_first * scale
    roots = [complex(np.exp(2j * math.pi * j / SWEEPS)) for j in range(1, SWEEPS)]
    return [(1.0 - relaxation - root) / beta for root in roots], beta**REACH * scale


def constants():
    basis_z, freq_z = real_basis(NZ)
    basis_y, freq_y = real_basis(NY)
    wave_z = 2.0 * np.cos(2.0 * math.pi * freq_z / NZ)
    wave_y = 2.0 * np.cos(2.0 * math.pi * freq_y / NY)
    mu = (couple_cross / couple_first) * (wave_y[:, None] + wave_z[None, :])
    mu = mu.reshape(ROWS, HALF, PAIR, LANE).transpose(0, 2, 1, 3)
    mu = np.tile(mu.reshape(GROUP, HALF, LANE), (1, PAIR, 1)).astype(np.float32)
    zf = np.stack(halves(basis_z.T))
    zb = np.stack(halves(basis_z))
    yh, yl = halves(basis_y)
    yf = np.concatenate([yh, yh, yl], axis=1)
    yh, yl = halves(basis_y.T)
    yb = np.concatenate([yh, yh, yl], axis=1)
    table = []
    for k in range(1, STEPS // 2):
        factors, last = mode_factors(k)
        for value in factors + [last]:
            table += [value.real, value.imag]
    for k in (0, STEPS // 2):
        factors, last = mode_factors(k)
        for value in factors[:2]:
            table += [value.real, value.imag**2]
        table += [factors[2].real, last.real]
    gamma = alpha_value ** (np.arange(STEPS) / STEPS)
    table += list(gamma) + list(1.0 / (STEPS * gamma))
    return mu, zf, zb, np.stack([yf, yb]), np.asarray(table, np.float32)


def split(value):
    high = value.astype(jnp.bfloat16)
    low = (value - high.astype(jnp.float32)).astype(jnp.bfloat16)
    return high, low


def dot(a, b):
    return jnp.dot(a, b, preferred_element_type=jnp.float32)


def rfft(x):
    n = len(x)
    if n == 2:
        return [(x[0] + x[1], None), (x[0] - x[1], None)]
    even, odd = rfft(x[0::2]), rfft(x[1::2])
    h, q = n // 2, n // 4
    out = [None] * (h + 1)
    out[0] = (even[0][0] + odd[0][0], None)
    out[h] = (even[0][0] - odd[0][0], None)
    out[q] = (even[q][0], -odd[q][0])
    for k in range(1, q):
        c, s = math.cos(2.0 * math.pi * k / n), -math.sin(2.0 * math.pi * k / n)
        er, ei = even[k]
        pr, pi = odd[k]
        tr, ti = c * pr - s * pi, c * pi + s * pr
        out[k] = (er + tr, ei + ti)
        out[h - k] = (er - tr, ti - ei)
    return out


def irfft(modes):
    n = 2 * (len(modes) - 1)
    if n == 2:
        return [modes[0][0] + modes[1][0], modes[0][0] - modes[1][0]]
    h, q = n // 2, n // 4
    even, odd = [None] * (q + 1), [None] * (q + 1)
    even[0] = (modes[0][0] + modes[h][0], None)
    odd[0] = (modes[0][0] - modes[h][0], None)
    even[q] = (2.0 * modes[q][0], None)
    odd[q] = (-2.0 * modes[q][1], None)
    for k in range(1, q):
        c, s = math.cos(2.0 * math.pi * k / n), math.sin(2.0 * math.pi * k / n)
        ar, ai = modes[k]
        br, bi = modes[h - k]
        even[k] = (ar + br, ai - bi)
        dr, di = ar - br, ai + bi
        odd[k] = (c * dr - s * di, c * di + s * dr)
    out = [None] * n
    out[0::2], out[1::2] = irfft(even), irfft(odd)
    return out


def kernel(
    state, initial, mu_all, zf_all, zb_all, ymat_all, table_all,
    updated, residual,
    st, late, res, upd, fore, third, mid, mid3, spec, back, ret, mu_ref, zf, zb, ymat, table,
    load_sem, own_sem, out_sem, edge_send, edge_recv, slab_send, slab_recv,
    fore_send, fore_recv, third_send, third_recv, halo_send, halo_recv, back_send, back_recv,
):
    tm, sp = lax.axis_index("tm"), lax.axis_index("space")
    pair, z = sp // DEPTH, lax.rem(sp, DEPTH)
    up, down = lax.rem(sp + 1, RING), lax.rem(sp + RING - 1, RING)
    above = pair * DEPTH + lax.rem(z + 1, DEPTH)
    below = pair * DEPTH + lax.rem(z + DEPTH - 1, DEPTH)
    both = pl.ds(1, 2)

    def remote(src, dst, send, recv, device):
        return pltpu.make_async_remote_copy(
            src_ref=src, dst_ref=dst, send_sem=send, recv_sem=recv,
            device_id=device, device_id_type=MESH,
        )

    def member(o):
        bit = [lax.rem(o // 2**i, 2) for i in range(5)]
        t = jnp.bitwise_xor(tm, bit[0] + 8 * bit[2] + 2 * bit[3] + 4 * bit[4])
        p = lax.rem(pair + bit[1], PAIR)
        return t, p, (t, p * DEPTH + z)

    nears = (up, down, above, below)
    barrier = pltpu.get_barrier_semaphore()
    for near in nears:
        pl.semaphore_signal(barrier, inc=1, device_id=(tm, near), device_id_type=MESH)

    @pl.loop(1, GROUP)
    def _(o):
        pl.semaphore_signal(barrier, inc=1, device_id=member(o)[2], device_id_type=MESH)

    loads = [
        pltpu.make_async_copy(src, dst, load_sem.at[i])
        for i, (src, dst) in enumerate(
            (
                (state, st.at[both, pl.ds(1, SLAB)]), (ymat_all, ymat), (zf_all, zf),
                (table_all, table), (mu_all, mu_ref), (zb_all, zb),
            )
        )
    ]
    for copy in loads:
        copy.start()

    @pl.when(tm == 0)
    def _():
        first = pltpu.make_async_copy(initial, st.at[0, pl.ds(1, SLAB)], own_sem.at[0])
        first.start()
        first.wait()

    odd = lax.rem(tm, 2) == 1
    extra = jnp.logical_and(odd, tm < ROWS - 1)
    later = jnp.logical_and(jnp.logical_not(odd), tm > 0)

    @pl.when(later)
    def _():
        @pl.loop(0, SLAB)
        def _(x):
            st[0, x + 1] = jnp.zeros((NY, NZ), jnp.float32)

    for copy in loads:
        copy.wait()

    edges = [
        remote(st.at[both, SLAB], st.at[both, 0], edge_send.at[0], edge_recv.at[0], (tm, up)),
        remote(st.at[both, 1], st.at[both, SLAB + 1], edge_send.at[1], edge_recv.at[1], (tm, down)),
    ]
    slab, slab_later = (
        remote(
            st.at[2, pl.ds(1, SLAB)], to, slab_send.at[0], slab_recv.at[0],
            (lax.rem(tm + 1, ROWS), sp),
        )
        for to in (st.at[0, pl.ds(1, SLAB)], late)
    )
    pl.semaphore_wait(barrier, GROUP - 1 + len(nears))
    for copy in edges:
        copy.start()

    @pl.when(jnp.logical_not(odd))
    def _():
        slab.start()

    def residual_of(step, x):
        s = st[step + 1, x + 1]
        near = st[step + 1, x] + st[step + 1, x + 2]
        cross = (
            pltpu.roll(s, 1, 0) + pltpu.roll(s, NY - 1, 0)
            + pltpu.roll(s, 1, 1) + pltpu.roll(s, NZ - 1, 1)
        )
        laplace = couple_first * (near - 2.0 * s) + couple_cross * (cross - 4.0 * s)
        return st[step, x + 1] - s + laplace + time_step * (s - s * s * s)

    def along_y(which, value):
        high, low = split(value)
        return dot(ymat[which], jnp.concatenate([high, low, high], axis=0))

    def along_z(matrix, value):
        high, low = split(value)
        return dot(high, matrix[0]) + dot(low, matrix[0]) + dot(high, matrix[1])

    def part_of(p):
        return pl.ds(pl.multiple_of(HALF * p, HALF), HALF)

    def landing_fore(phase, t, p):
        step, steps, place, places = PHASES[phase]
        return mid.at[pl.ds(step, steps), t, pl.ds(place, places), part_of(p)]

    def leaving_fore(phase, t, p):
        step, steps, place, places = PHASES[phase]
        return fore.at[t * PAIR + p, pl.ds(step, steps), pl.ds(place, places)]

    def own_fore(phase):
        return pltpu.make_async_copy(
            leaving_fore(phase, tm, pair), landing_fore(phase, tm, pair), own_sem.at[phase]
        )

    def send_fore(phase):
        @pl.loop(1, GROUP)
        def _(o):
            t, p, device = member(o)
            remote(
                leaving_fore(phase, t, p), landing_fore(phase, tm, pair),
                fore_send.at[phase], fore_recv.at[phase, o], device,
            ).start()

        own_fore(phase).start()

    def landing_third(t, p):
        return mid3.at[t // 2, :, part_of(p)]

    def own_third():
        return pltpu.make_async_copy(
            third.at[tm * PAIR + pair], landing_third(tm, pair), own_sem.at[3 + CHUNKS]
        )

    def lay_out(target, place, rows):
        for j in range(2):
            for g in range(GROUP):
                r0, c0 = j * NY + (g // PAIR) * HALF, (g % PAIR) * LANE
                target(g, place + j, rows[r0 : r0 + HALF, c0 : c0 + LANE])

    def work(step, place):
        rows = []
        for j in range(2):
            x = lax.rem(place + j + 1, SLAB)
            value = residual_of(step, x)
            res[step, x] = value
            rows.append(along_y(0, value))
        rows = along_z(zf, jnp.concatenate(rows, axis=0)) * table[GAMMA + 2 * tm + step]

        def put(g, at, value):
            fore[g, step, at] = value

        lay_out(put, place, rows)

    def work_third(place):
        rows = [along_y(0, st[2, lax.rem(place + j + 1, SLAB) + 1]) for j in range(2)]
        rows = along_z(zf, jnp.concatenate(rows, axis=0)) * table[GAMMA + 2 * tm + 2]

        def put(g, at, value):
            third[g, at] = value

        lay_out(put, place, rows)

    @pl.loop(0, OWN - 1)
    def _(i):
        work(1, 2 * i)

    @pl.when(z == 0)
    def _():
        edges[0].wait_recv()

    @pl.when(z == DEPTH - 1)
    def _():
        edges[1].wait_recv()

    send_fore(0)

    @pl.when(extra)
    def _():
        @pl.loop(0, OWN)
        def _(i):
            work_third(2 * i)

        @pl.loop(1, GROUP)
        def _(o):
            t, p, device = member(o)
            remote(
                third.at[t * PAIR + p], landing_third(tm, pair),
                third_send.at[0], third_recv.at[tm // 2, pair], device,
            ).start()

        own_third().start()

    @pl.when(odd)
    def _():
        slab.wait_recv()

    @pl.loop(0, OWN - 1)
    def _(i):
        work(0, 2 * i)

    send_fore(1)

    @pl.when(z != 0)
    def _():
        edges[0].wait_recv()

    @pl.when(z != DEPTH - 1)
    def _():
        edges[1].wait_recv()

    @pl.loop(0, 2)
    def _(step):
        work(step, SLAB - 2)

    send_fore(2)

    def halo_copies(phase, times=pl.ds(0, ROWS)):
        step, steps, place, places = PHASES[phase]
        copies = []
        for way, near, first, last, to in (
            (0, above, SLAB - REACH - 1, SLAB - 1, SLAB),
            (1, below, 0, REACH - 1, SLAB + REACH + 1),
            (2, below, SLAB - 1, SLAB, SLAB + REACH),
        ):
            at, end = max(first, place), min(last, place + places)
            if at < end:
                copies.append(
                    remote(
                        mid.at[pl.ds(step, steps), times, pl.ds(at, end - at)],
                        mid.at[pl.ds(step, steps), times, pl.ds(to + at - first, end - at)],
                        halo_send.at[phase, way], halo_recv.at[phase, way], (tm, near),
                    )
                )
        return copies

    def wait_third(chip):
        for p in range(PAIR):
            source = 2 * chip - 1
            own = jnp.logical_and(tm == source, pair == p)

            @pl.when(own)
            def _():
                own_third().wait()

            @pl.when(jnp.logical_not(own))
            def _():
                landing = landing_third(source, p)
                remote(
                    landing, landing, third_send.at[0], third_recv.at[source // 2, p],
                    (source, p * DEPTH + z),
                ).wait_recv()

    for phase, (step, steps, place, places) in enumerate(PHASES):
        own_fore(phase).wait()
        here = pl.ds(place, places)

        @pl.loop(0, GROUP // BATCH)
        def _(i):
            @pl.loop(0, BATCH)
            def _(j):
                o = i * BATCH + j

                @pl.when(o > 0)
                def _():
                    t, p, device = member(o)
                    landing = landing_fore(phase, t, p)
                    remote(
                        landing, landing, fore_send.at[phase], fore_recv.at[phase, o], device
                    ).wait_recv()

            chip = member(i * BATCH)[0] // 2
            if step == 0:
                @pl.when(chip > 0)
                def _():
                    if place == 0:
                        wait_third(chip)
                    mid[0, 2 * chip, here] = mid[0, 2 * chip, here] + mid3[chip - 1, here]

            for copy in halo_copies(phase, pl.ds(2 * chip, 2)):
                copy.start()

    @pl.when(extra)
    def _():
        slab_later.start()

    @pl.loop(0, WIDE)
    def _(i):
        @pl.when(i == SLAB)
        def _():
            for phase in range(len(PHASES)):
                for copy in halo_copies(phase):
                    copy.wait_recv()

        before, after = jnp.logical_and(i >= SLAB, i < SLAB + REACH), i >= SLAB + REACH
        x = jnp.where(i < SLAB, REACH + lax.rem(i + 1, SLAB), jnp.where(before, i - SLAB, i))
        turned = jnp.logical_or(
            jnp.logical_and(before, z == 0), jnp.logical_and(after, z == DEPTH - 1)
        )
        modes = rfft([mid[n % 2, n // 2, i] for n in range(STEPS)])
        slots = [modes[0][0], modes[STEPS // 2][0]]
        for k in range(1, STEPS // 2):
            slots += [modes[k][0], modes[k][1]]
        for slot, value in enumerate(slots):
            spec[slot, x] = jnp.where(turned, pltpu.roll(value, HALF, 0), value)

    mu = mu_ref[tm * PAIR + pair]

    @pl.loop(0, 2)
    def _(slot):
        base = REAL + slot * SWEEPS
        v = [spec[slot, x] for x in range(WIDE)]
        for j in (0, 1):
            dr, square = mu + table[base + 2 * j], table[base + 2 * j + 1]
            first = [v[x - 1] + v[x + 1] + dr * v[x] for x in range(1, len(v) - 1)]
            v = [
                first[x - 1] + first[x + 1] + dr * first[x] + square * v[x + 1]
                for x in range(1, len(first) - 1)
            ]
        dr = mu + table[base + 4]
        v = [v[x - 1] + v[x + 1] + dr * v[x] for x in range(1, len(v) - 1)]
        for x in range(SLAB):
            spec[slot, x] = table[base + 5] * v[x]

    @pl.loop(1, STEPS // 2)
    def _(k):
        base = (k - 1) * 2 * SWEEPS
        vr = [spec[2 * k, x] for x in range(WIDE)]
        vi = [spec[2 * k + 1, x] for x in range(WIDE)]
        for j in range(REACH):
            dr, di = mu + table[base + 2 * j], table[base + 2 * j + 1]
            inner = range(1, len(vr) - 1)
            vr, vi = (
                [vr[x - 1] + vr[x + 1] + dr * vr[x] - di * vi[x] for x in inner],
                [vi[x - 1] + vi[x + 1] + dr * vi[x] + di * vr[x] for x in inner],
            )
        lr, li = table[base + 2 * REACH], table[base + 2 * REACH + 1]
        for x in range(SLAB):
            spec[2 * k, x] = lr * vr[x] - li * vi[x]
            spec[2 * k + 1, x] = lr * vi[x] + li * vr[x]

    part = SLAB // CHUNKS

    def planes_of(chunk):
        return pl.ds(pl.multiple_of(chunk * part, part), part)

    def leaving(chunk, t, p):
        return back.at[t, :, planes_of(chunk), part_of(p)]

    def landing_back(chunk, t, p):
        return ret.at[t * PAIR + p, :, planes_of(chunk)]

    def own_back(chunk):
        return pltpu.make_async_copy(
            leaving(chunk, tm, pair), landing_back(chunk, tm, pair), own_sem.at[3 + chunk]
        )

    @pl.loop(0, CHUNKS)
    def _(chunk):
        @pl.loop(0, part)
        def _(i):
            x = chunk * part + i
            modes = [(spec[0, x], None)]
            modes += [(spec[2 * k, x], spec[2 * k + 1, x]) for k in range(1, STEPS // 2)]
            modes += [(spec[1, x], None)]
            values = irfft(modes)
            for n in range(STEPS):
                back[n // 2, n % 2, x] = values[n]

        @pl.loop(1, GROUP)
        def _(o):
            t, p, device = member(o)
            remote(
                leaving(chunk, t, p), landing_back(chunk, tm, pair),
                back_send.at[chunk], back_recv.at[chunk, o], device,
            ).start()

        own_back(chunk).start()

    @pl.when(later)
    def _():
        slab_later.wait_recv()

        @pl.loop(0, SLAB)
        def _(x):
            res[0, x] = res[0, x] + late[x]

    out_res = pltpu.make_async_copy(res, residual, out_sem.at[0])
    out_res.start()

    def out_upd(chunk):
        xs = planes_of(chunk)
        return pltpu.make_async_copy(upd.at[:, xs], updated.at[:, xs], out_sem.at[1 + chunk])

    @pl.loop(0, CHUNKS)
    def _(chunk):
        own_back(chunk).wait()

        @pl.loop(1, GROUP)
        def _(o):
            t, p, device = member(o)
            landing = landing_back(chunk, t, p)
            remote(
                landing, landing, back_send.at[chunk], back_recv.at[chunk, o], device
            ).wait_recv()

        @pl.loop(0, part)
        def _(i):
            step, x0 = i // (part // 2), chunk * part + 2 * lax.rem(i, part // 2)
            rows = []
            for j in range(2):
                for r in range(ROWS):
                    rows.append(
                        jnp.concatenate([ret[r * PAIR + p, step, x0 + j] for p in range(PAIR)], axis=1)
                    )
            value = along_z(zb, jnp.concatenate(rows, axis=0))
            scale = table[GAMMA + STEPS + 2 * tm + step]
            for j in range(2):
                delta = along_y(1, value[j * NY : (j + 1) * NY])
                upd[step, x0 + j] = st[step + 1, x0 + j + 1] + scale * delta

        out_upd(chunk).start()

    for copy in edges:
        copy.wait_send()

    @pl.when(tm < ROWS - 1)
    def _():
        slab.wait_send()

    others = pl.ds(0, GROUP - 1)

    @pl.when(extra)
    def _():
        sent = third.at[others]
        remote(sent, sent, third_send.at[0], third_recv.at[0, 0], (tm, above)).wait_send()

    for phase, (step, steps, place, places) in enumerate(PHASES):
        for copy in halo_copies(phase):
            copy.wait_send()
        sent = fore.at[others, pl.ds(step, steps), pl.ds(place, places)]
        remote(sent, sent, fore_send.at[phase], fore_recv.at[phase, 0], (tm, above)).wait_send()
    for chunk in range(CHUNKS):
        sent = ret.at[others, :, planes_of(chunk)]
        remote(sent, sent, back_send.at[chunk], back_recv.at[chunk, 0], (tm, above)).wait_send()
        out_upd(chunk).wait()
    out_res.wait()


def body(state, initial):
    mu, zf, zb, ymat, table = (jnp.asarray(c) for c in constants())
    whole = jax.ShapeDtypeStruct(state.shape, jnp.float32)
    steps = STEPS // ROWS
    hbm = pl.BlockSpec(memory_space=pltpu.HBM)
    f32 = jnp.float32
    return pl.pallas_call(
        kernel,
        out_shape=(whole, whole),
        in_specs=[hbm] * 7,
        out_specs=(hbm, hbm),
        scratch_shapes=[
            pltpu.VMEM((steps + 1, SLAB + 2, NY, NZ), f32),
            pltpu.VMEM((SLAB, NY, NZ), f32),
            pltpu.VMEM((steps, SLAB, NY, NZ), f32),
            pltpu.VMEM((steps, SLAB, NY, NZ), f32),
            pltpu.VMEM((GROUP, steps, SLAB, HALF, LANE), f32),
            pltpu.VMEM((GROUP, SLAB, HALF, LANE), f32),
            pltpu.VMEM((steps, ROWS, WIDE, SUB, LANE), f32),
            pltpu.VMEM((ROWS // 2, SLAB, SUB, LANE), f32),
            pltpu.VMEM((STEPS, WIDE, SUB, LANE), f32),
            pltpu.VMEM((ROWS, steps, SLAB, SUB, LANE), f32),
            pltpu.VMEM((GROUP, steps, SLAB, HALF, LANE), f32),
            pltpu.VMEM(mu.shape, f32),
            pltpu.VMEM(zf.shape, jnp.bfloat16),
            pltpu.VMEM(zb.shape, jnp.bfloat16),
            pltpu.VMEM(ymat.shape, jnp.bfloat16),
            pltpu.SMEM(table.shape, f32),
            pltpu.SemaphoreType.DMA((6,)),
            pltpu.SemaphoreType.DMA((4 + CHUNKS,)),
            pltpu.SemaphoreType.DMA((1 + CHUNKS,)),
            pltpu.SemaphoreType.DMA((2,)),
            pltpu.SemaphoreType.DMA((2,)),
            pltpu.SemaphoreType.DMA((1,)),
            pltpu.SemaphoreType.DMA((1,)),
            pltpu.SemaphoreType.DMA((len(PHASES),)),
            pltpu.SemaphoreType.DMA((len(PHASES), GROUP)),
            pltpu.SemaphoreType.DMA((1,)),
            pltpu.SemaphoreType.DMA((ROWS // 2, PAIR)),
            pltpu.SemaphoreType.DMA((len(PHASES), 3)),
            pltpu.SemaphoreType.DMA((len(PHASES), 3)),
            pltpu.SemaphoreType.DMA((CHUNKS,)),
            pltpu.SemaphoreType.DMA((CHUNKS, GROUP)),
        ],
        compiler_params=pltpu.CompilerParams(
            collective_id=0, has_side_effects=True, vmem_limit_bytes=60 * 2**20
        ),
        cost_estimate=pl.CostEstimate(flops=10**9, bytes_accessed=8 * 2**20, transcendentals=0),
    )(state, initial, mu, zf, zb, ymat, table)


def solution(mesh):
    in_specs = (P("tm", "space", None, None), P("space", None, None))
    out_specs = (P("tm", "space", None, None), P("tm", "space", None, None))
    return jax.shard_map(body, mesh=mesh, in_specs=in_specs, out_specs=out_specs, check_vma=False)
```

```python
import math

import jax
import jax.numpy as jnp
import ml_dtypes
import numpy as np
from jax import lax
from jax.experimental import pallas as pl
from jax.experimental.pallas import tpu as pltpu
from jax.sharding import PartitionSpec as P

MESH = pl.DeviceIdType.MESH
SWEEPS = 6
STEPS, NX, NY, NZ = 32, 128, 64, 256
ROWS = 16
RING = 16
PAIR, DEPTH = 2, 8
GROUP = ROWS * PAIR
SLAB = NX // RING
REACH = SWEEPS - 1
WIDE = SLAB + 2 * REACH
SUB, LANE = 8, 128
HALF = SUB // PAIR
REAL = (STEPS // 2 - 1) * 2 * SWEEPS
GAMMA = REAL + 2 * SWEEPS
CHUNKS = 4
OWN = SLAB // 2
PHASES = ((1, 1, 0, SLAB - 2), (0, 1, 0, SLAB - 2), (0, 2, SLAB - 2, 2))
BATCH = 2 * PAIR

alpha_value = 0.1
time_step = 0.1
couple_first = 0.4
couple_cross = 0.05
reaction_shift = 0.1
relaxation = 0.9
rho = alpha_value ** (1.0 / STEPS)


def real_basis(n):
    cells = np.arange(n)
    rows, freq = np.zeros((n, n)), np.zeros(n)
    rows[0] = 1.0 / math.sqrt(n)
    rows[1] = (-1.0) ** cells / math.sqrt(n)
    freq[1] = n // 2
    for k in range(1, n // 2):
        angle = 2.0 * math.pi * (k * cells % n) / n
        rows[2 * k] = math.sqrt(2.0 / n) * np.cos(angle)
        rows[2 * k + 1] = math.sqrt(2.0 / n) * np.sin(angle)
        freq[2 * k] = freq[2 * k + 1] = k
    return rows, freq


def halves(matrix):
    high = matrix.astype(ml_dtypes.bfloat16)
    low = (matrix - high.astype(np.float64)).astype(ml_dtypes.bfloat16)
    return high, low


def mode_factors(k):
    theta = 2.0 * math.pi * k / STEPS
    diag = 1.0 + reaction_shift + 2.0 * couple_first + 4.0 * couple_cross
    shift = complex(diag - rho * math.cos(theta), rho * math.sin(theta))
    scale = relaxation / shift
    beta = couple_first * scale
    roots = [complex(np.exp(2j * math.pi * j / SWEEPS)) for j in range(1, SWEEPS)]
    return [(1.0 - relaxation - root) / beta for root in roots], beta**REACH * scale


def constants():
    basis_z, freq_z = real_basis(NZ)
    basis_y, freq_y = real_basis(NY)
    wave_z = 2.0 * np.cos(2.0 * math.pi * freq_z / NZ)
    wave_y = 2.0 * np.cos(2.0 * math.pi * freq_y / NY)
    mu = (couple_cross / couple_first) * (wave_y[:, None] + wave_z[None, :])
    mu = mu.reshape(ROWS, HALF, PAIR, LANE).transpose(0, 2, 1, 3)
    mu = np.tile(mu.reshape(GROUP, HALF, LANE), (1, PAIR, 1)).astype(np.float32)
    zf = np.stack(halves(basis_z.T))
    zb = np.stack(halves(basis_z))
    yh, yl = halves(basis_y)
    yf = np.concatenate([yh, yh, yl], axis=1)
    yh, yl = halves(basis_y.T)
    yb = np.concatenate([yh, yh, yl], axis=1)
    table = []
    for k in range(1, STEPS // 2):
        factors, last = mode_factors(k)
        for value in factors + [last]:
            table += [value.real, value.imag]
    for k in (0, STEPS // 2):
        factors, last = mode_factors(k)
        for value in factors[:2]:
            table += [value.real, value.imag**2]
        table += [factors[2].real, last.real]
    gamma = alpha_value ** (np.arange(STEPS) / STEPS)
    table += list(gamma) + list(1.0 / (STEPS * gamma))
    return mu, zf, zb, np.stack([yf, yb]), np.asarray(table, np.float32)


def split(value):
    high = value.astype(jnp.bfloat16)
    low = (value - high.astype(jnp.float32)).astype(jnp.bfloat16)
    return high, low


def dot(a, b):
    return jnp.dot(a, b, preferred_element_type=jnp.float32)


def rfft(x):
    n = len(x)
    if n == 2:
        return [(x[0] + x[1], None), (x[0] - x[1], None)]
    even, odd = rfft(x[0::2]), rfft(x[1::2])
    h, q = n // 2, n // 4
    out = [None] * (h + 1)
    out[0] = (even[0][0] + odd[0][0], None)
    out[h] = (even[0][0] - odd[0][0], None)
    out[q] = (even[q][0], -odd[q][0])
    for k in range(1, q):
        c, s = math.cos(2.0 * math.pi * k / n), -math.sin(2.0 * math.pi * k / n)
        er, ei = even[k]
        pr, pi = odd[k]
        tr, ti = c * pr - s * pi, c * pi + s * pr
        out[k] = (er + tr, ei + ti)
        out[h - k] = (er - tr, ti - ei)
    return out


def irfft(modes):
    n = 2 * (len(modes) - 1)
    if n == 2:
        return [modes[0][0] + modes[1][0], modes[0][0] - modes[1][0]]
    h, q = n // 2, n // 4
    even, odd = [None] * (q + 1), [None] * (q + 1)
    even[0] = (modes[0][0] + modes[h][0], None)
    odd[0] = (modes[0][0] - modes[h][0], None)
    even[q] = (2.0 * modes[q][0], None)
    odd[q] = (-2.0 * modes[q][1], None)
    for k in range(1, q):
        c, s = math.cos(2.0 * math.pi * k / n), math.sin(2.0 * math.pi * k / n)
        ar, ai = modes[k]
        br, bi = modes[h - k]
        even[k] = (ar + br, ai - bi)
        dr, di = ar - br, ai + bi
        odd[k] = (c * dr - s * di, c * di + s * dr)
    out = [None] * n
    out[0::2], out[1::2] = irfft(even), irfft(odd)
    return out


def kernel(
    state, initial, mu_all, zf_all, zb_all, ymat_all, table_all,
    updated, residual,
    st, late, res, upd, fore, third, mid, mid3, spec, back, ret, mu_ref, zf, zb, ymat, table,
    load_sem, own_sem, out_sem, edge_send, edge_recv, slab_send, slab_recv,
    fore_send, fore_recv, third_send, third_recv, halo_send, halo_recv, back_send, back_recv,
):
    tm, sp = lax.axis_index("tm"), lax.axis_index("space")
    pair, z = sp // DEPTH, lax.rem(sp, DEPTH)
    up, down = lax.rem(sp + 1, RING), lax.rem(sp + RING - 1, RING)
    above = pair * DEPTH + lax.rem(z + 1, DEPTH)
    below = pair * DEPTH + lax.rem(z + DEPTH - 1, DEPTH)
    both = pl.ds(1, 2)

    def remote(src, dst, send, recv, device):
        return pltpu.make_async_remote_copy(
            src_ref=src, dst_ref=dst, send_sem=send, recv_sem=recv,
            device_id=device, device_id_type=MESH,
        )

    def member(o):
        bit = [lax.rem(o // 2**i, 2) for i in range(5)]
        t = jnp.bitwise_xor(tm, bit[0] + 8 * bit[2] + 2 * bit[3] + 4 * bit[4])
        p = lax.rem(pair + bit[1], PAIR)
        return t, p, (t, p * DEPTH + z)

    nears = (up, down, above, below)
    barrier = pltpu.get_barrier_semaphore()
    for near in nears:
        pl.semaphore_signal(barrier, inc=1, device_id=(tm, near), device_id_type=MESH)

    @pl.loop(1, GROUP)
    def _(o):
        pl.semaphore_signal(barrier, inc=1, device_id=member(o)[2], device_id_type=MESH)

    loads = [
        pltpu.make_async_copy(src, dst, load_sem.at[i])
        for i, (src, dst) in enumerate(
            (
                (state, st.at[both, pl.ds(1, SLAB)]), (ymat_all, ymat), (zf_all, zf),
                (table_all, table), (mu_all, mu_ref), (zb_all, zb),
            )
        )
    ]
    for copy in loads:
        copy.start()

    @pl.when(tm == 0)
    def _():
        first = pltpu.make_async_copy(initial, st.at[0, pl.ds(1, SLAB)], own_sem.at[0])
        first.start()
        first.wait()

    odd = lax.rem(tm, 2) == 1
    extra = jnp.logical_and(odd, tm < ROWS - 1)
    later = jnp.logical_and(jnp.logical_not(odd), tm > 0)

    @pl.when(later)
    def _():
        @pl.loop(0, SLAB)
        def _(x):
            st[0, x + 1] = jnp.zeros((NY, NZ), jnp.float32)

    for copy in loads:
        copy.wait()

    edges = [
        remote(st.at[both, SLAB], st.at[both, 0], edge_send.at[0], edge_recv.at[0], (tm, up)),
        remote(st.at[both, 1], st.at[both, SLAB + 1], edge_send.at[1], edge_recv.at[1], (tm, down)),
    ]
    slab, slab_later = (
        remote(
            st.at[2, pl.ds(1, SLAB)], to, slab_send.at[0], slab_recv.at[0],
            (lax.rem(tm + 1, ROWS), sp),
        )
        for to in (st.at[0, pl.ds(1, SLAB)], late)
    )
    pl.semaphore_wait(barrier, GROUP - 1 + len(nears))
    for copy in edges:
        copy.start()

    @pl.when(jnp.logical_not(odd))
    def _():
        slab.start()

    def residual_of(step, x):
        s = st[step + 1, x + 1]
        near = st[step + 1, x] + st[step + 1, x + 2]
        cross = (
            pltpu.roll(s, 1, 0) + pltpu.roll(s, NY - 1, 0)
            + pltpu.roll(s, 1, 1) + pltpu.roll(s, NZ - 1, 1)
        )
        laplace = couple_first * (near - 2.0 * s) + couple_cross * (cross - 4.0 * s)
        rest = st[step, x + 1] + laplace + time_step * (s - s * s * s)
        return rest - s, rest

    def along_y(which, value):
        high, low = split(value)
        return dot(ymat[which], jnp.concatenate([high, low, high], axis=0))

    def along_z(matrix, value):
        high, low = split(value)
        return dot(high, matrix[0]) + dot(low, matrix[0]) + dot(high, matrix[1])

    def part_of(p):
        return pl.ds(pl.multiple_of(HALF * p, HALF), HALF)

    def landing_fore(phase, t, p):
        step, steps, place, places = PHASES[phase]
        return mid.at[pl.ds(step, steps), t, pl.ds(place, places), part_of(p)]

    def leaving_fore(phase, t, p):
        step, steps, place, places = PHASES[phase]
        return fore.at[t * PAIR + p, pl.ds(step, steps), pl.ds(place, places)]

    def own_fore(phase):
        return pltpu.make_async_copy(
            leaving_fore(phase, tm, pair), landing_fore(phase, tm, pair), own_sem.at[phase]
        )

    def send_fore(phase):
        @pl.loop(1, GROUP)
        def _(o):
            t, p, device = member(o)
            remote(
                leaving_fore(phase, t, p), landing_fore(phase, tm, pair),
                fore_send.at[phase], fore_recv.at[phase, o], device,
            ).start()

        own_fore(phase).start()

    def landing_third(t, p):
        return mid3.at[t // 2, :, part_of(p)]

    def own_third():
        return pltpu.make_async_copy(
            third.at[tm * PAIR + pair], landing_third(tm, pair), own_sem.at[3 + CHUNKS]
        )

    def lay_out(target, place, rows):
        for j in range(2):
            for g in range(GROUP):
                r0, c0 = j * NY + (g // PAIR) * HALF, (g % PAIR) * LANE
                target(g, place + j, rows[r0 : r0 + HALF, c0 : c0 + LANE])

    def work(step, place):
        rows = []
        for j in range(2):
            x = lax.rem(place + j + 1, SLAB)
            value, rest = residual_of(step, x)
            res[step, x] = rest
            rows.append(along_y(0, value))
        rows = along_z(zf, jnp.concatenate(rows, axis=0)) * table[GAMMA + 2 * tm + step]

        def put(g, at, value):
            fore[g, step, at] = value

        lay_out(put, place, rows)

    def work_third(place):
        rows = [along_y(0, st[2, lax.rem(place + j + 1, SLAB) + 1]) for j in range(2)]
        rows = along_z(zf, jnp.concatenate(rows, axis=0)) * table[GAMMA + 2 * tm + 2]

        def put(g, at, value):
            third[g, at] = value

        lay_out(put, place, rows)

    @pl.loop(0, OWN - 1)
    def _(i):
        work(1, 2 * i)

    @pl.when(z == 0)
    def _():
        edges[0].wait_recv()

    @pl.when(z == DEPTH - 1)
    def _():
        edges[1].wait_recv()

    send_fore(0)

    @pl.when(extra)
    def _():
        @pl.loop(0, OWN)
        def _(i):
            work_third(2 * i)

        @pl.loop(1, GROUP)
        def _(o):
            t, p, device = member(o)
            remote(
                third.at[t * PAIR + p], landing_third(tm, pair),
                third_send.at[0], third_recv.at[tm // 2, pair], device,
            ).start()

        own_third().start()

    @pl.when(odd)
    def _():
        slab.wait_recv()

    @pl.loop(0, OWN - 1)
    def _(i):
        work(0, 2 * i)

    send_fore(1)

    @pl.when(z != 0)
    def _():
        edges[0].wait_recv()

    @pl.when(z != DEPTH - 1)
    def _():
        edges[1].wait_recv()

    @pl.loop(0, 2)
    def _(step):
        work(step, SLAB - 2)

    send_fore(2)

    def halo_copies(phase, times=pl.ds(0, ROWS)):
        step, steps, place, places = PHASES[phase]
        copies = []
        for way, near, first, last, to in (
            (0, above, SLAB - REACH - 1, SLAB - 1, SLAB),
            (1, below, 0, REACH - 1, SLAB + REACH + 1),
            (2, below, SLAB - 1, SLAB, SLAB + REACH),
        ):
            at, end = max(first, place), min(last, place + places)
            if at < end:
                copies.append(
                    remote(
                        mid.at[pl.ds(step, steps), times, pl.ds(at, end - at)],
                        mid.at[pl.ds(step, steps), times, pl.ds(to + at - first, end - at)],
                        halo_send.at[phase, way], halo_recv.at[phase, way], (tm, near),
                    )
                )
        return copies

    def wait_third(chip):
        for p in range(PAIR):
            source = 2 * chip - 1
            own = jnp.logical_and(tm == source, pair == p)

            @pl.when(own)
            def _():
                own_third().wait()

            @pl.when(jnp.logical_not(own))
            def _():
                landing = landing_third(source, p)
                remote(
                    landing, landing, third_send.at[0], third_recv.at[source // 2, p],
                    (source, p * DEPTH + z),
                ).wait_recv()

    for phase, (step, steps, place, places) in enumerate(PHASES):
        own_fore(phase).wait()
        here = pl.ds(place, places)

        @pl.loop(0, GROUP // BATCH)
        def _(i):
            @pl.loop(0, BATCH)
            def _(j):
                o = i * BATCH + j

                @pl.when(o > 0)
                def _():
                    t, p, device = member(o)
                    landing = landing_fore(phase, t, p)
                    remote(
                        landing, landing, fore_send.at[phase], fore_recv.at[phase, o], device
                    ).wait_recv()

            chip = member(i * BATCH)[0] // 2
            if step == 0:
                @pl.when(chip > 0)
                def _():
                    if place == 0:
                        wait_third(chip)
                    mid[0, 2 * chip, here] = mid[0, 2 * chip, here] + mid3[chip - 1, here]

            for copy in halo_copies(phase, pl.ds(2 * chip, 2)):
                copy.start()

    @pl.when(extra)
    def _():
        slab_later.start()

    @pl.loop(0, WIDE)
    def _(i):
        @pl.when(i == SLAB)
        def _():
            for phase in range(len(PHASES)):
                for copy in halo_copies(phase):
                    copy.wait_recv()

        before, after = jnp.logical_and(i >= SLAB, i < SLAB + REACH), i >= SLAB + REACH
        x = jnp.where(i < SLAB, REACH + lax.rem(i + 1, SLAB), jnp.where(before, i - SLAB, i))
        turned = jnp.logical_or(
            jnp.logical_and(before, z == 0), jnp.logical_and(after, z == DEPTH - 1)
        )
        modes = rfft([mid[n % 2, n // 2, i] for n in range(STEPS)])
        slots = [modes[0][0], modes[STEPS // 2][0]]
        for k in range(1, STEPS // 2):
            slots += [modes[k][0], modes[k][1]]
        for slot, value in enumerate(slots):
            spec[slot, x] = jnp.where(turned, pltpu.roll(value, HALF, 0), value)

    mu = mu_ref[tm * PAIR + pair]

    @pl.loop(0, 2)
    def _(slot):
        base = REAL + slot * SWEEPS
        v = [spec[slot, x] for x in range(WIDE)]
        for j in (0, 1):
            dr, square = mu + table[base + 2 * j], table[base + 2 * j + 1]
            first = [v[x - 1] + v[x + 1] + dr * v[x] for x in range(1, len(v) - 1)]
            v = [
                first[x - 1] + first[x + 1] + dr * first[x] + square * v[x + 1]
                for x in range(1, len(first) - 1)
            ]
        dr = mu + table[base + 4]
        v = [v[x - 1] + v[x + 1] + dr * v[x] for x in range(1, len(v) - 1)]
        for x in range(SLAB):
            spec[slot, x] = table[base + 5] * v[x]

    @pl.loop(1, STEPS // 2)
    def _(k):
        base = (k - 1) * 2 * SWEEPS
        vr = [spec[2 * k, x] for x in range(WIDE)]
        vi = [spec[2 * k + 1, x] for x in range(WIDE)]
        for j in range(REACH):
            dr, di = mu + table[base + 2 * j], table[base + 2 * j + 1]
            inner = range(1, len(vr) - 1)
            vr, vi = (
                [vr[x - 1] + vr[x + 1] + dr * vr[x] - di * vi[x] for x in inner],
                [vi[x - 1] + vi[x + 1] + dr * vi[x] + di * vr[x] for x in inner],
            )
        lr, li = table[base + 2 * REACH], table[base + 2 * REACH + 1]
        for x in range(SLAB):
            spec[2 * k, x] = lr * vr[x] - li * vi[x]
            spec[2 * k + 1, x] = lr * vi[x] + li * vr[x]

    part = SLAB // CHUNKS

    def planes_of(chunk):
        return pl.ds(pl.multiple_of(chunk * part, part), part)

    def leaving(chunk, t, p):
        return back.at[t, :, planes_of(chunk), part_of(p)]

    def landing_back(chunk, t, p):
        return ret.at[t * PAIR + p, :, planes_of(chunk)]

    def own_back(chunk):
        return pltpu.make_async_copy(
            leaving(chunk, tm, pair), landing_back(chunk, tm, pair), own_sem.at[3 + chunk]
        )

    @pl.loop(0, CHUNKS)
    def _(chunk):
        @pl.loop(0, part)
        def _(i):
            x = chunk * part + i
            modes = [(spec[0, x], None)]
            modes += [(spec[2 * k, x], spec[2 * k + 1, x]) for k in range(1, STEPS // 2)]
            modes += [(spec[1, x], None)]
            values = irfft(modes)
            for n in range(STEPS):
                back[n // 2, n % 2, x] = values[n]

        @pl.loop(1, GROUP)
        def _(o):
            t, p, device = member(o)
            remote(
                leaving(chunk, t, p), landing_back(chunk, tm, pair),
                back_send.at[chunk], back_recv.at[chunk, o], device,
            ).start()

        own_back(chunk).start()

    @pl.when(later)
    def _():
        slab_later.wait_recv()

        @pl.loop(0, SLAB)
        def _(x):
            res[0, x] = res[0, x] + late[x]

    out_res = pltpu.make_async_copy(res, residual, out_sem.at[0])
    out_res.start()

    def out_upd(chunk):
        xs = planes_of(chunk)
        return pltpu.make_async_copy(upd.at[:, xs], updated.at[:, xs], out_sem.at[1 + chunk])

    @pl.loop(0, CHUNKS)
    def _(chunk):
        own_back(chunk).wait()

        @pl.loop(1, GROUP)
        def _(o):
            t, p, device = member(o)
            landing = landing_back(chunk, t, p)
            remote(
                landing, landing, back_send.at[chunk], back_recv.at[chunk, o], device
            ).wait_recv()

        @pl.loop(0, part)
        def _(i):
            step, x0 = i // (part // 2), chunk * part + 2 * lax.rem(i, part // 2)
            rows = []
            for j in range(2):
                for r in range(ROWS):
                    rows.append(
                        jnp.concatenate([ret[r * PAIR + p, step, x0 + j] for p in range(PAIR)], axis=1)
                    )
            value = along_z(zb, jnp.concatenate(rows, axis=0))
            scale = table[GAMMA + STEPS + 2 * tm + step]
            for j in range(2):
                delta = along_y(1, value[j * NY : (j + 1) * NY])
                upd[step, x0 + j] = scale * delta

        out_upd(chunk).start()

    for copy in edges:
        copy.wait_send()

    @pl.when(tm < ROWS - 1)
    def _():
        slab.wait_send()

    others = pl.ds(0, GROUP - 1)

    @pl.when(extra)
    def _():
        sent = third.at[others]
        remote(sent, sent, third_send.at[0], third_recv.at[0, 0], (tm, above)).wait_send()

    for phase, (step, steps, place, places) in enumerate(PHASES):
        for copy in halo_copies(phase):
            copy.wait_send()
        sent = fore.at[others, pl.ds(step, steps), pl.ds(place, places)]
        remote(sent, sent, fore_send.at[phase], fore_recv.at[phase, 0], (tm, above)).wait_send()
    for chunk in range(CHUNKS):
        sent = ret.at[others, :, planes_of(chunk)]
        remote(sent, sent, back_send.at[chunk], back_recv.at[chunk, 0], (tm, above)).wait_send()
        out_upd(chunk).wait()
    out_res.wait()


def body(state, initial):
    mu, zf, zb, ymat, table = (jnp.asarray(c) for c in constants())
    whole = jax.ShapeDtypeStruct(state.shape, jnp.float32)
    steps = STEPS // ROWS
    hbm = pl.BlockSpec(memory_space=pltpu.HBM)
    f32 = jnp.float32
    delta, rest = pl.pallas_call(
        kernel,
        out_shape=(whole, whole),
        in_specs=[hbm] * 7,
        out_specs=(hbm, hbm),
        scratch_shapes=[
            pltpu.VMEM((steps + 1, SLAB + 2, NY, NZ), f32),
            pltpu.VMEM((SLAB, NY, NZ), f32),
            pltpu.VMEM((steps, SLAB, NY, NZ), f32),
            pltpu.VMEM((steps, SLAB, NY, NZ), f32),
            pltpu.VMEM((GROUP, steps, SLAB, HALF, LANE), f32),
            pltpu.VMEM((GROUP, SLAB, HALF, LANE), f32),
            pltpu.VMEM((steps, ROWS, WIDE, SUB, LANE), f32),
            pltpu.VMEM((ROWS // 2, SLAB, SUB, LANE), f32),
            pltpu.VMEM((STEPS, WIDE, SUB, LANE), f32),
            pltpu.VMEM((ROWS, steps, SLAB, SUB, LANE), f32),
            pltpu.VMEM((GROUP, steps, SLAB, HALF, LANE), f32),
            pltpu.VMEM(mu.shape, f32),
            pltpu.VMEM(zf.shape, jnp.bfloat16),
            pltpu.VMEM(zb.shape, jnp.bfloat16),
            pltpu.VMEM(ymat.shape, jnp.bfloat16),
            pltpu.SMEM(table.shape, f32),
            pltpu.SemaphoreType.DMA((6,)),
            pltpu.SemaphoreType.DMA((4 + CHUNKS,)),
            pltpu.SemaphoreType.DMA((1 + CHUNKS,)),
            pltpu.SemaphoreType.DMA((2,)),
            pltpu.SemaphoreType.DMA((2,)),
            pltpu.SemaphoreType.DMA((1,)),
            pltpu.SemaphoreType.DMA((1,)),
            pltpu.SemaphoreType.DMA((len(PHASES),)),
            pltpu.SemaphoreType.DMA((len(PHASES), GROUP)),
            pltpu.SemaphoreType.DMA((1,)),
            pltpu.SemaphoreType.DMA((ROWS // 2, PAIR)),
            pltpu.SemaphoreType.DMA((len(PHASES), 3)),
            pltpu.SemaphoreType.DMA((len(PHASES), 3)),
            pltpu.SemaphoreType.DMA((CHUNKS,)),
            pltpu.SemaphoreType.DMA((CHUNKS, GROUP)),
        ],
        compiler_params=pltpu.CompilerParams(
            collective_id=0, has_side_effects=True, vmem_limit_bytes=60 * 2**20
        ),
        cost_estimate=pl.CostEstimate(flops=10**9, bytes_accessed=8 * 2**20, transcendentals=0),
    )(state, initial, mu, zf, zb, ymat, table)
    return state + delta, rest - state


def solution(mesh):
    in_specs = (P("tm", "space", None, None), P("space", None, None))
    out_specs = (P("tm", "space", None, None), P("tm", "space", None, None))
    return jax.shard_map(body, mesh=mesh, in_specs=in_specs, out_specs=out_specs, check_vma=False)
```
